32 devices in a mesh: cells: 8 (over z, y), rank: 4 (over x, core).
Axes of the slice: x: 2, y: 2, z: 4, core: 2. Of those that a mesh axis runs over, the one named last changes fastest.
Arguments:
- x_emb: bfloat16 [4096, 256], P('cells'), may hold values from -40 to 40, as said below
- y_emb: bfloat16 [4096, 256], P('cells'), may hold values from -40 to 40, as said below
- q_factor: float32 [4096, 512], P('cells', 'rank'), may hold values from 0 to 45, as said below
- r_factor: float32 [4096, 512], P('cells', 'rank'), may hold values from 0 to 45, as said below
- g_weights: float32 [512], P('rank'), may hold values from 2048 to 8192
- a_mass: float32 [4096], P('cells'), may hold values from 128 to 512
- b_mass: float32 [4096], P('cells'), may hold values from 128 to 512
- expr: bfloat16 [4096, 2048], P('cells', 'rank'), may hold values from -9 to 9, as said below
Outputs:
- q_new: float32 [4096, 512], P('cells', 'rank')
- r_new: float32 [4096, 512], P('cells', 'rank')
- rank_share: float32 [512], P('rank')
- predicted: bfloat16 [4096, 2048], P('cells', 'rank')
The draws below stay inside these ranges and needn't reach their ends.
Inputs may be any that keep to these rules, and one draw needn't show every extreme that they name: `x_emb`: finite embedding values. `y_emb`: finite embedding values. `q_factor`: every entry is positive. `r_factor`: every entry is positive. `expr`: finite expression values.
All inputs are finite; a program needn't handle non-finite values. Where the reference program divides by a largest or mean magnitude, that divisor is 1e-20 or more.
Results may differ from the reference program's by a relative error of at most 0.0075.
Values may be sent and summed in bfloat16 or wider, within the bound.
A program may use at most 64 MiB of HBM per device.

```python
import math
import jax
import jax.numpy as jnp

DIM = 256
RANK = 512
GENES = 2048
PASSES = 10
CELLS = 4096


def ramp_factor(count):
    ramp = jnp.arange(count, dtype=jnp.float32) / max(count - 1, 1)
    return 1.0 + 2.0 * ramp


def embedding_rows(key, offset):
    rows = ramp_factor(CELLS)
    base = jnp.clip(jax.random.normal(key, (CELLS, DIM), jnp.float32), -6.0, 6.0)
    jitter = jnp.exp(jax.random.uniform(jax.random.fold_in(key, 5), (CELLS,), jnp.float32, -0.4, 0.4))
    values = (base + offset) * (rows * jitter)[:, None]
    return jnp.clip(values, -40.0, 40.0)


def draw_x_emb(key, part):
    return embedding_rows(jax.random.fold_in(key, 11), 0.0).astype(jnp.bfloat16)


def draw_y_emb(key, part):
    offset = jax.random.uniform(jax.random.fold_in(key, 23), (DIM,), jnp.float32, -1.0, 1.0)
    return embedding_rows(jax.random.fold_in(key, 29), offset[None, :]).astype(jnp.bfloat16)


def cluster_labels(key, salt):
    return jax.random.randint(jax.random.fold_in(key, salt), (CELLS,), 0, RANK)


def factor_entries(key, salt):
    labels = cluster_labels(key, salt)
    member = (labels[:, None] == jnp.arange(RANK)[None, :]).astype(jnp.float32)
    rows = ramp_factor(CELLS)
    noise = jax.random.uniform(jax.random.fold_in(key, salt + 1), (CELLS, RANK), jnp.float32, 0.25, 1.0)
    return noise * (1.0 + 4.0 * member) * rows[:, None]


def draw_q_factor(key, part):
    return factor_entries(key, 101)


def draw_r_factor(key, part):
    return factor_entries(key, 201)


def draw_expr(key, part):
    labels = cluster_labels(key, 201)
    profile = jnp.clip(jax.random.normal(jax.random.fold_in(key, 301), (RANK, GENES), jnp.float32), -6.0, 6.0)
    noise = 0.5 * jnp.clip(jax.random.normal(jax.random.fold_in(key, 302), (CELLS, GENES), jnp.float32), -6.0, 6.0)
    return (profile[labels] + noise).astype(jnp.bfloat16)


def levels(stream_key, extent, shards, smallest, largest):
    def one(position, shards_of):
        steps = jax.random.uniform(jax.random.fold_in(jax.random.fold_in(stream_key, 6), position), (shards_of,), jnp.float32, smallest / len(shards), largest / len(shards))
        return jnp.repeat(jnp.exp(steps), extent[position] // shards_of).reshape((-1,) + (1,) * (len(extent) - position - 1))

    loudness = one(*shards[0])
    for cut in shards[1:]:
        loudness = loudness * one(*cut)
    return loudness


def setup_inputs(seed: int = 0) -> dict:
    seeds = jax.random.split(jax.random.key(seed), 9)
    x_emb = draw_x_emb(jax.random.fold_in(seeds[8], 71), 0)
    y_emb = draw_y_emb(jax.random.fold_in(seeds[8], 71), 0)
    q_factor = draw_q_factor(jax.random.fold_in(seeds[8], 71), 0)
    r_factor = draw_r_factor(jax.random.fold_in(seeds[8], 71), 0)
    g_weights = jnp.clip(jnp.exp(math.log(8192.0) - 1.3862944 * jax.random.uniform(seeds[4], (RANK,), jnp.float32) ** levels(seeds[4], (RANK,), ((0, 4),), -0.2, 0.2)), 2048.0, 8192.0)
    a_mass = jnp.clip(jnp.exp(math.log(512.0) - 1.3862944 * jax.random.uniform(seeds[5], (CELLS,), jnp.float32) ** levels(seeds[5], (CELLS,), ((0, 8),), -0.2, 0.2)), 128.0, 512.0)
    b_mass = jnp.clip(jnp.exp(math.log(512.0) - 1.3862944 * jax.random.uniform(seeds[6], (CELLS,), jnp.float32) ** levels(seeds[6], (CELLS,), ((0, 8),), -0.2, 0.2)), 128.0, 512.0)
    expr = draw_expr(jax.random.fold_in(seeds[8], 71), 0)
    return dict(x_emb=x_emb, y_emb=y_emb, q_factor=q_factor, r_factor=r_factor, g_weights=g_weights, a_mass=a_mass, b_mass=b_mass, expr=expr)


SCALE = 0.0625
GAMMA = 10.0
POWER = 0.8


def reference(x_emb, y_emb, q_factor, r_factor, g_weights, a_mass, b_mass, expr):
    norms_one = jnp.sum(jnp.square(x_emb.astype(jnp.float32)), axis=1)
    norms_two = jnp.sum(jnp.square(y_emb.astype(jnp.float32)), axis=1)
    q_round = q_factor.astype(jnp.bfloat16)
    r_round = r_factor.astype(jnp.bfloat16)
    cross_xq = jnp.dot(x_emb.T, q_round, preferred_element_type=jnp.float32)
    cross_yr = jnp.dot(y_emb.T, r_round, preferred_element_type=jnp.float32)
    xq_vec = jnp.sum(norms_one[:, None] * q_factor, axis=0)
    cq_vec = jnp.sum(q_factor, axis=0)
    yr_vec = jnp.sum(norms_two[:, None] * r_factor, axis=0)
    cr_vec = jnp.sum(r_factor, axis=0)
    grad_q = SCALE * (norms_one[:, None] * cr_vec[None, :] + yr_vec[None, :]
                      - 2.0 * jnp.dot(x_emb, cross_yr.astype(jnp.bfloat16), preferred_element_type=jnp.float32)) / g_weights[None, :]
    grad_r = SCALE * (norms_two[:, None] * cq_vec[None, :] + xq_vec[None, :]
                      - 2.0 * jnp.dot(y_emb, cross_xq.astype(jnp.bfloat16), preferred_element_type=jnp.float32)) / g_weights[None, :]
    curvature = SCALE * (xq_vec * cr_vec + cq_vec * yr_vec - 2.0 * jnp.sum(cross_xq * cross_yr, axis=0))
    grad_g = -curvature / jnp.square(g_weights)
    peak = jnp.maximum(jnp.max(jnp.abs(grad_q)), jnp.maximum(jnp.max(jnp.abs(grad_r)), jnp.max(jnp.abs(grad_g))))
    eta = GAMMA / (peak + 1e-6)
    kern_q = q_factor * jnp.exp(-eta * grad_q)
    kern_r = r_factor * jnp.exp(-eta * grad_r)
    kern_g = g_weights * jnp.exp(-eta * grad_g)
    v_q = jnp.ones((RANK,), jnp.float32)
    v_r = jnp.ones((RANK,), jnp.float32)
    u_q = jnp.ones((CELLS,), jnp.float32)
    u_r = jnp.ones((CELLS,), jnp.float32)
    weights = kern_g
    for step in range(PASSES):
        s_q = jnp.sum(kern_q * v_q[None, :], axis=1)
        s_r = jnp.sum(kern_r * v_r[None, :], axis=1)
        u_q = (a_mass / s_q) ** POWER
        u_r = (b_mass / s_r) ** POWER
        t_q = jnp.sum(kern_q * u_q[:, None], axis=0)
        t_r = jnp.sum(kern_r * u_r[:, None], axis=0)
        weights = jnp.exp((jnp.log(kern_g) + jnp.log(v_q * t_q) + jnp.log(v_r * t_r)) / 3.0)
        v_q = weights / t_q
        v_r = weights / t_r
    q_new = u_q[:, None] * kern_q * v_q[None, :]
    r_new = u_r[:, None] * kern_r * v_r[None, :]
    row_mass = jnp.sum(q_new, axis=1)
    scaled = (q_new / weights[None, :]).astype(jnp.bfloat16)
    profiles = jnp.dot(r_new.astype(jnp.bfloat16).T, expr, preferred_element_type=jnp.float32)
    mixed = jnp.dot(scaled, profiles.astype(jnp.bfloat16), preferred_element_type=jnp.float32)
    predicted = (mixed / row_mass[:, None]).astype(jnp.bfloat16)
    return q_new, r_new, weights / CELLS, predicted
```

```python
import functools

import jax
import jax.numpy as jnp
from jax import lax
from jax.experimental import pallas as pl
from jax.experimental.pallas import tpu as pltpu
from jax.sharding import PartitionSpec as P

PASSES = 10
SCALE = 0.0625
GAMMA = 10.0
POWER = 0.8
LANES = 128
MESH = pl.DeviceIdType.MESH
F32 = jnp.float32
BF16 = jnp.bfloat16


def dot(left, right):
    return jnp.dot(left, right, preferred_element_type=F32)


def contract_rows(left, right):
    return lax.dot_general(
        left, right, (((0,), (0,)), ((), ())), preferred_element_type=F32
    )


def wide(rows, first, count):
    return jnp.concatenate([rows[first + i : first + i + 1] for i in range(count)], axis=1)


def tall(*rows):
    return jnp.concatenate(
        [row[:, i * LANES : (i + 1) * LANES] for row in rows for i in range(row.shape[1] // LANES)],
        axis=0,
    )


def row_product(row, matrix):
    high = row.astype(BF16).astype(F32)
    low = row - high
    shape = (16, row.shape[1])
    index = lax.broadcasted_iota(jnp.int32, shape, 0)
    parts = jnp.where(
        index == 0,
        jnp.broadcast_to(high, shape),
        jnp.where(index == 1, jnp.broadcast_to(low, shape), 0.0),
    )
    out = dot(parts.astype(BF16), matrix)
    return out[0:1] + out[1:2]


def as_column(row):
    return jnp.transpose(jnp.broadcast_to(row, (LANES, row.shape[1])))


def pick_row(rows, index):
    position = lax.broadcasted_iota(jnp.int32, rows.shape, 0)
    return jnp.sum(jnp.where(position == index, rows, 0.0), axis=0, keepdims=True)


def kernel(
    n, ranks, owners, tiles, cells_total,
    x_ref, y_ref, q_ref, r_ref, g_ref, a_ref, b_ref, expr_ref,
    q_out, r_out, w_out, pred_out,
    factors, part_src, part_buf, cross, vec_buf, vecs, grads_q, grads_r, grads_g,
    peaks, kq, kr, kqt, krt, t_buf, prof_src, prof_buf, prof,
    part_send, part_recv, vec_send, vec_recv, cross_send, cross_recv,
    fac_send, fac_recv, rank_send, rank_recv, vr_send, vr_recv,
    peak_send, peak_recv, t_send, t_recv, prof_send, prof_recv, gat_send, gat_recv,
):
    me = lax.axis_index("cells")
    k = lax.axis_index("rank")
    near = k + 1 - 2 * lax.rem(k, 2)
    far = lax.rem(k + 2, 4)
    across = 3 - k

    def peers(body):
        if n <= 8:
            for offset in range(1, n):
                body(lax.rem(me + offset, n))
        else:
            def one(offset, carry):
                body(lax.rem(me + offset, n))
                return carry
            lax.fori_loop(1, n, one, 0)

    def only(limit, index, body):
        if limit >= n:
            body()
        else:
            pl.when(index < limit)(body)

    def to_peer(src, dst, send, recv, j):
        return pltpu.make_async_remote_copy(
            src_ref=src, dst_ref=dst, send_sem=send, recv_sem=recv,
            device_id=(j, k), device_id_type=MESH,
        )

    def to_rank(src, dst, send, recv, other):
        return pltpu.make_async_remote_copy(
            src_ref=src, dst_ref=dst, send_sem=send, recv_sem=recv,
            device_id=(me, other), device_id_type=MESH,
        )

    barrier = pltpu.get_barrier_semaphore()
    peers(lambda j: pl.semaphore_signal(barrier, inc=1, device_id=(j, k), device_id_type=MESH))
    for other in (near, far, across):
        pl.semaphore_signal(barrier, inc=1, device_id=(me, other), device_id_type=MESH)

    x, y = x_ref[...], y_ref[...]
    q, r = q_ref[...], r_ref[...]
    q_round, r_round = q.astype(BF16), r.astype(BF16)
    factors[k, 0] = q_round
    factors[k, 1] = r_round
    depth = part_src.shape[2]
    part_src[:, 0] = contract_rows(x, q_round).astype(BF16).reshape(owners, depth, LANES)
    part_src[:, 1] = contract_rows(y, r_round).astype(BF16).reshape(owners, depth, LANES)
    norms_one = jnp.sum(jnp.square(x.astype(F32)), axis=1, keepdims=True)
    norms_two = jnp.sum(jnp.square(y.astype(F32)), axis=1, keepdims=True)
    vec_buf[me] = jnp.concatenate(
        [
            jnp.sum(norms_one * q, axis=0, keepdims=True),
            jnp.sum(q, axis=0, keepdims=True),
            jnp.sum(norms_two * r, axis=0, keepdims=True),
            jnp.sum(r, axis=0, keepdims=True),
            jnp.zeros((4, LANES), F32),
        ],
        axis=0,
    )
    pl.semaphore_wait(barrier, n - 1 + 3)

    def part_copy(j, slot):
        return to_peer(part_src.at[lax.rem(j, owners)], part_buf.at[slot], part_send.at[j], part_recv.at[slot], j)

    def vec_copy(j, slot):
        return to_peer(vec_buf.at[me], vec_buf.at[slot], vec_send.at[j], vec_recv.at[slot], j)

    def send_parts(j):
        only(owners, j, lambda: part_copy(j, me).start())
        vec_copy(j, me).start()

    peers(send_parts)

    def factor_copy(slot, i, other):
        return to_rank(factors.at[slot], factors.at[slot], fac_send.at[i], fac_recv.at[i], other)

    factor_copy(k, 0, near).start()
    factor_copy(k, 1, far).start()

    def own_part():
        part_buf[me] = part_src[me]

    only(owners, me, own_part)

    def reduce_parts():
        peers(lambda j: part_copy(j, j).wait_recv())
        total = part_buf[0].astype(F32)
        for j in range(1, n):
            total = total + part_buf[j].astype(F32)
        cross[k, me] = total.astype(BF16)

    only(owners, me, reduce_parts)

    def cross_copy(j, slot):
        return to_peer(cross.at[k, slot], cross.at[k, slot], cross_send.at[j], cross_recv.at[slot], j)

    only(owners, me, lambda: peers(lambda j: cross_copy(j, me).start()))

    peers(lambda j: vec_copy(j, j).wait_recv())
    vec = vec_buf[0]
    for j in range(1, n):
        vec = vec + vec_buf[j]
    slot_row = lax.broadcasted_iota(jnp.int32, (8, LANES), 0)
    vecs[k] = jnp.where(slot_row == 4, jnp.broadcast_to(g_ref[...], (8, LANES)), vec)

    def vecs_copy(slot, i, other):
        return to_rank(vecs.at[slot], vecs.at[slot], vr_send.at[i], vr_recv.at[i], other)

    for i, other in enumerate((near, far, across)):
        vecs_copy(k, i, other).start()
    factor_copy(far, 1, far).wait_recv()
    factor_copy(far, 2, near).start()

    peers(lambda j: only(owners, j, lambda: cross_copy(j, j).wait_recv()))

    def rank_copy(slot, i, other):
        return to_rank(cross.at[slot], cross.at[slot], rank_send.at[i], rank_recv.at[i], other)

    rank_copy(k, 1, far).start()
    rank_copy(k, 0, near).start()

    def gradients(kk):
        info = vecs[kk]
        xq_vec, cq_vec, yr_vec, cr_vec, g = (info[i : i + 1] for i in range(5))
        scale = SCALE / g
        dim = x.shape[1]
        cross_xq = cross[kk, :, 0].reshape(dim, LANES)
        cross_yr = cross[kk, :, 1].reshape(dim, LANES)
        grad_q = (norms_one * cr_vec + yr_vec - 2.0 * dot(x, cross_yr)) * scale
        grad_r = (norms_two * cq_vec + xq_vec - 2.0 * dot(y, cross_xq)) * scale
        grads_q[kk] = grad_q
        grads_r[kk] = grad_r
        inner = jnp.sum(cross_xq.astype(F32) * cross_yr.astype(F32), axis=0, keepdims=True)
        curvature = SCALE * (xq_vec * cr_vec + cq_vec * yr_vec - 2.0 * inner)
        grad_g = -curvature / jnp.square(g)
        grads_g[kk] = jnp.broadcast_to(grad_g, (8, LANES))
        return jnp.maximum(
            jnp.max(jnp.maximum(jnp.abs(grad_q), jnp.abs(grad_r)), axis=0, keepdims=True),
            jnp.abs(grad_g),
        )

    peak = gradients(k)
    vecs_copy(near, 0, near).wait_recv()
    rank_copy(near, 0, near).wait_recv()
    peak = jnp.maximum(peak, gradients(near))
    rank_copy(far, 1, far).wait_recv()
    rank_copy(far, 2, near).start()
    vecs_copy(far, 1, far).wait_recv()
    peak = jnp.maximum(peak, gradients(far))
    vecs_copy(across, 2, across).wait_recv()
    rank_copy(across, 2, near).wait_recv()
    peak = jnp.maximum(peak, gradients(across))
    peaks[me] = jnp.broadcast_to(peak, (8, LANES))

    def peak_copy(j, slot):
        return to_peer(peaks.at[me], peaks.at[slot], peak_send.at[j], peak_recv.at[slot], j)

    peers(lambda j: peak_copy(j, me).start())
    factor_copy(near, 0, near).wait_recv()
    factor_copy(across, 2, near).wait_recv()
    log_a, log_b = jnp.log(a_ref[...]), jnp.log(b_ref[...])
    peers(lambda j: peak_copy(j, j).wait_recv())
    top = peaks[0]
    for j in range(1, n):
        top = jnp.maximum(top, peaks[j])
    eta = GAMMA / (jnp.max(top, axis=1, keepdims=True)[0:1] + 1e-6)

    log_g = []
    for kk in range(ranks):
        columns = slice(kk * LANES, (kk + 1) * LANES)
        kern_q = factors[kk, 0].astype(F32) * jnp.exp(-eta * grads_q[kk])
        kern_r = factors[kk, 1].astype(F32) * jnp.exp(-eta * grads_r[kk])
        kq[:, columns] = kern_q.astype(BF16)
        kr[:, columns] = kern_r.astype(BF16)
        kqt[columns, :] = jnp.transpose(kern_q).astype(BF16)
        krt[columns, :] = jnp.transpose(kern_r).astype(BF16)
        log_g.append(jnp.log(vecs[kk][4:5]) - eta * grads_g[kk][0:1])
    log_kern_g = jnp.concatenate(log_g + log_g, axis=0)

    def t_copy(parity, j, slot):
        return to_peer(
            t_buf.at[parity, me], t_buf.at[parity, slot],
            t_send.at[parity, j], t_recv.at[parity, slot], j,
        )

    def one_pass(step, carry):
        v, _, _, _, _ = carry
        parity = lax.rem(step, 2)
        s_q = row_product(wide(v, 0, ranks), kqt[...])
        s_r = row_product(wide(v, ranks, ranks), krt[...])
        u_q = jnp.exp(POWER * (log_a - jnp.log(s_q)))
        u_r = jnp.exp(POWER * (log_b - jnp.log(s_r)))
        t_buf[parity, me] = tall(row_product(u_q, kq[...]), row_product(u_r, kr[...]))
        peers(lambda j: t_copy(parity, j, me).start())
        peers(lambda j: t_copy(parity, j, j).wait_recv())
        t = t_buf[parity, 0]
        for j in range(1, n):
            t = t + t_buf[parity, j]
        peers(lambda j: t_copy(parity, j, j).wait_send())
        logs = jnp.log(v * t)
        other = jnp.concatenate([logs[ranks:], logs[:ranks]], axis=0)
        weights = jnp.exp((log_kern_g + logs + other) / 3.0)
        return weights / t, weights, t, u_q, u_r

    ones = jnp.ones((2 * ranks, LANES), F32)
    row = jnp.ones((1, x.shape[0]), F32)
    v, weights, t, u_q, u_r = lax.fori_loop(
        0, PASSES, one_pass, (ones, ones, ones, row, row)
    )

    share = prof_src.shape[1]
    left = (krt[...].astype(F32) * u_r).astype(BF16)
    prof_src[...] = dot(left, expr_ref[...]).astype(BF16).reshape(prof_src.shape)

    def prof_copy(j, slot):
        return to_peer(prof_src.at[lax.rem(j, tiles)], prof_buf.at[slot], prof_send.at[j], prof_recv.at[slot], j)

    peers(lambda j: only(tiles, j, lambda: prof_copy(j, me).start()))

    def own_prof():
        prof_buf[me] = prof_src[me]

    only(tiles, me, own_prof)

    w_out[...] = pick_row(weights, k) / cells_total
    own_q = q_ref[...] * jnp.exp(-eta * grads_q[k])
    own_r = r_ref[...] * jnp.exp(-eta * grads_r[k])
    q_out[...] = as_column(u_q) * own_q * pick_row(v, k)
    r_out[...] = as_column(u_r) * own_r * pick_row(v, k + ranks)
    inverse = as_column(1.0 / row_product(wide(v, 0, ranks), kqt[...]))
    scaled = (kq[...].astype(F32) * wide(v[ranks:] / t[:ranks], 0, ranks)).astype(BF16)

    def gather_copy(j, slot):
        return to_peer(prof.at[slot], prof.at[slot], gat_send.at[j], gat_recv.at[slot], j)

    def reduce_prof():
        peers(lambda j: prof_copy(j, j).wait_recv())
        total = prof_buf[0].astype(F32)
        for j in range(1, n):
            total = total + prof_buf[j].astype(F32)
        prof[me] = total.astype(BF16)
        peers(lambda j: gather_copy(j, me).start())

    only(tiles, me, reduce_prof)
    peers(lambda j: only(tiles, j, lambda: gather_copy(j, j).wait_recv()))
    mixed = dot(scaled, prof[...].reshape(tiles * share, prof.shape[2]))
    for i in range(mixed.shape[1] // LANES):
        columns = slice(i * LANES, (i + 1) * LANES)
        pred_out[:, columns] = (mixed[:, columns] * inverse).astype(BF16)

    def sends(j):
        only(owners, j, lambda: part_copy(j, j).wait_send())
        vec_copy(j, j).wait_send()
        only(owners, me, lambda: cross_copy(j, me).wait_send())
        peak_copy(j, j).wait_send()
        only(tiles, j, lambda: prof_copy(j, j).wait_send())
        only(tiles, me, lambda: gather_copy(j, me).wait_send())

    peers(sends)
    for i, (slot, other) in enumerate(((k, near), (k, far), (far, near))):
        factor_copy(slot, i, other).wait_send()
        rank_copy(slot, i, other).wait_send()
    for i, other in enumerate((near, far, across)):
        vecs_copy(k, i, other).wait_send()


def shards(n, ranks, x_emb, y_emb, q_factor, r_factor, g_weights, a_mass, b_mass, expr):
    rows, dim = x_emb.shape
    genes = expr.shape[1]
    rank_all = ranks * LANES
    owners = min(n, dim // 16)
    tiles = min(n, rank_all // 16)
    vmem = pl.BlockSpec(memory_space=pltpu.VMEM)
    dma = pltpu.SemaphoreType.DMA
    pair = [dma((n,)), dma((n,))]
    three = [dma((3,)), dma((3,))]
    q_new, r_new, rank_share, predicted = pl.pallas_call(
        functools.partial(kernel, n, ranks, owners, tiles, float(rows * n)),
        out_shape=(
            jax.ShapeDtypeStruct(q_factor.shape, F32),
            jax.ShapeDtypeStruct(r_factor.shape, F32),
            jax.ShapeDtypeStruct((1, LANES), F32),
            jax.ShapeDtypeStruct((rows, genes), BF16),
        ),
        in_specs=[vmem] * 8,
        out_specs=(vmem,) * 4,
        scratch_shapes=[
            pltpu.VMEM((ranks, 2, rows, LANES), BF16),
            pltpu.VMEM((owners, 2, dim // owners, LANES), BF16),
            pltpu.VMEM((n, 2, dim // owners, LANES), BF16),
            pltpu.VMEM((ranks, owners, 2, dim // owners, LANES), BF16),
            pltpu.VMEM((n, 8, LANES), F32),
            pltpu.VMEM((ranks, 8, LANES), F32),
            pltpu.VMEM((ranks, rows, LANES), F32),
            pltpu.VMEM((ranks, rows, LANES), F32),
            pltpu.VMEM((ranks, 8, LANES), F32),
            pltpu.VMEM((n, 8, LANES), F32),
            pltpu.VMEM((rows, rank_all), BF16),
            pltpu.VMEM((rows, rank_all), BF16),
            pltpu.VMEM((rank_all, rows), BF16),
            pltpu.VMEM((rank_all, rows), BF16),
            pltpu.VMEM((2, n, 8, LANES), F32),
            pltpu.VMEM((tiles, rank_all // tiles, genes), BF16),
            pltpu.VMEM((n, rank_all // tiles, genes), BF16),
            pltpu.VMEM((tiles, rank_all // tiles, genes), BF16),
        ]
        + pair + pair + pair + three + three + three + pair
        + [dma((2, n)), dma((2, n))]
        + pair + pair,
        compiler_params=pltpu.CompilerParams(
            collective_id=0, has_side_effects=True, vmem_limit_bytes=48 * 1024 * 1024
        ),
        cost_estimate=pl.CostEstimate(
            flops=2 * rows * (2 * dim * LANES + 2 * dim * rank_all + 2 * rank_all * genes),
            bytes_accessed=4 * 1024 * 1024,
            transcendentals=2 * rows * rank_all,
        ),
        name="transport_step",
    )(
        x_emb, y_emb, q_factor, r_factor, g_weights.reshape(1, LANES),
        a_mass.reshape(1, rows), b_mass.reshape(1, rows), expr,
    )
    return q_new, r_new, rank_share.reshape(LANES), predicted


def solution(mesh):
    n, ranks = mesh.shape["cells"], mesh.shape["rank"]
    assert ranks == 4
    return jax.shard_map(
        functools.partial(shards, n, ranks),
        mesh=mesh,
        in_specs=(
            P("cells", None),
            P("cells", None),
            P("cells", "rank"),
            P("cells", "rank"),
            P("rank"),
            P("cells"),
            P("cells"),
            P("cells", "rank"),
        ),
        out_specs=(P("cells", "rank"), P("cells", "rank"), P("rank"), P("cells", "rank")),
        check_vma=False,
    )
```

```python
import functools

import jax
import jax.numpy as jnp
from jax import lax
from jax.experimental import pallas as pl
from jax.experimental.pallas import tpu as pltpu
from jax.sharding import PartitionSpec as P

PASSES = 10
SCALE = 0.0625
GAMMA = 10.0
POWER = 0.8
LANES = 128
VMEM_LIMIT = 56 * 1024 * 1024
MESH = pl.DeviceIdType.MESH
F32 = jnp.float32
BF16 = jnp.bfloat16


def dot(left, right):
    return jnp.dot(left, right, preferred_element_type=F32)


def contract_rows(left, right):
    return lax.dot_general(
        left, right, (((0,), (0,)), ((), ())), preferred_element_type=F32
    )


def wide(rows, first, count):
    return jnp.concatenate([rows[first + i : first + i + 1] for i in range(count)], axis=1)


def tall(*rows):
    return jnp.concatenate(
        [row[:, i * LANES : (i + 1) * LANES] for row in rows for i in range(row.shape[1] // LANES)],
        axis=0,
    )


def row_product(row, matrix):
    high = row.astype(BF16).astype(F32)
    low = row - high
    shape = (16, row.shape[1])
    index = lax.broadcasted_iota(jnp.int32, shape, 0)
    parts = jnp.where(
        index == 0,
        jnp.broadcast_to(high, shape),
        jnp.where(index == 1, jnp.broadcast_to(low, shape), 0.0),
    )
    out = dot(parts.astype(BF16), matrix)
    return out[0:1] + out[1:2]


def as_column(row):
    return jnp.transpose(jnp.broadcast_to(row, (LANES, row.shape[1])))


def pick_row(rows, index):
    position = lax.broadcasted_iota(jnp.int32, rows.shape, 0)
    return jnp.sum(jnp.where(position == index, rows, 0.0), axis=0, keepdims=True)


def kernel(
    n, ranks, owners, tiles, cells_total,
    x_hbm, y_hbm, q_hbm, r_hbm, g_hbm, a_hbm, b_hbm, expr_hbm,
    q_hbm_out, r_hbm_out, w_hbm_out, pred_hbm_out,
    q_out, r_out, w_out, pred_out, out_sem,
    x_ref, y_ref, q_ref, r_ref, g_ref, a_ref, b_ref, expr_ref, in_sem,
    factors, part_src, part_buf, cross, vec_buf, vecs, grads_q, grads_r, grads_g,
    peaks, kq, kr, kqt, krt, t_buf, mate_kern, mate_expr, u_buf, scaled,
    prof_src, prof_buf, prof,
    part_send, part_recv, vec_send, vec_recv, cross_send, cross_recv,
    fac_send, fac_recv, rank_send, rank_recv, vr_send, vr_recv,
    peak_send, peak_recv, t_send, t_recv, mate_send, mate_recv,
    prof_send, prof_recv, gat_send, gat_recv, fwd_send, fwd_recv,
):
    me = lax.axis_index("cells")
    k = lax.axis_index("rank")
    near = k + 1 - 2 * lax.rem(k, 2)
    far = lax.rem(k + 2, 4)
    across = 3 - k
    group, half = me // 2, lax.rem(me, 2)
    groups = n // 2
    mate = me + 1 - 2 * half

    def each(first, last, body):
        if last - first <= 8:
            for i in range(first, last):
                body(i)
        else:
            def one(i, carry):
                body(i)
                return carry
            lax.fori_loop(first, last, one, 0)

    def peers(body):
        each(1, n, lambda offset: body(lax.rem(me + offset, n)))

    def lines(body):
        each(1, groups, lambda offset: body(lax.rem(group + offset, groups)))

    def only(limit, index, body, count=n):
        if limit >= count:
            body()
        else:
            pl.when(index < limit)(body)

    def to_peer(src, dst, send, recv, j):
        return pltpu.make_async_remote_copy(
            src_ref=src, dst_ref=dst, send_sem=send, recv_sem=recv,
            device_id=(j, k), device_id_type=MESH,
        )

    def to_rank(src, dst, send, recv, other):
        return pltpu.make_async_remote_copy(
            src_ref=src, dst_ref=dst, send_sem=send, recv_sem=recv,
            device_id=(me, other), device_id_type=MESH,
        )

    loads = [
        pltpu.make_async_copy(src, dst, in_sem.at[i])
        for i, (src, dst) in enumerate(
            (
                (q_hbm, q_ref), (x_hbm, x_ref), (r_hbm, r_ref), (y_hbm, y_ref),
                (g_hbm, g_ref), (a_hbm, a_ref), (b_hbm, b_ref), (expr_hbm, expr_ref),
            )
        )
    ]
    for load in loads:
        load.start()
    barrier = pltpu.get_barrier_semaphore()
    peers(lambda j: pl.semaphore_signal(barrier, inc=1, device_id=(j, k), device_id_type=MESH))
    for other in (near, far, across):
        pl.semaphore_signal(barrier, inc=1, device_id=(me, other), device_id_type=MESH)

    depth = part_src.shape[2]
    loads[0].wait()
    q = q_ref[...]
    q_round = q.astype(BF16)
    factors[k, 0] = q_round
    loads[1].wait()
    x = x_ref[...]
    part_src[:, 0] = contract_rows(x, q_round).astype(BF16).reshape(owners, depth, LANES)
    loads[2].wait()
    r = r_ref[...]
    r_round = r.astype(BF16)
    factors[k, 1] = r_round
    loads[3].wait()
    y = y_ref[...]
    part_src[:, 1] = contract_rows(y, r_round).astype(BF16).reshape(owners, depth, LANES)
    norms_one = jnp.sum(jnp.square(x.astype(F32)), axis=1, keepdims=True)
    norms_two = jnp.sum(jnp.square(y.astype(F32)), axis=1, keepdims=True)
    vec_buf[me] = jnp.concatenate(
        [
            jnp.sum(norms_one * q, axis=0, keepdims=True),
            jnp.sum(q, axis=0, keepdims=True),
            jnp.sum(norms_two * r, axis=0, keepdims=True),
            jnp.sum(r, axis=0, keepdims=True),
            jnp.zeros((4, LANES), F32),
        ],
        axis=0,
    )
    for load in loads[4:]:
        load.wait()
    pl.semaphore_wait(barrier, n - 1 + 3)

    def part_copy(j, slot):
        return to_peer(part_src.at[lax.rem(j, owners)], part_buf.at[slot], part_send.at[j], part_recv.at[slot], j)

    def vec_copy(j, slot):
        return to_peer(vec_buf.at[me], vec_buf.at[slot], vec_send.at[j], vec_recv.at[slot], j)

    def send_parts(j):
        only(owners, j, lambda: part_copy(j, me).start())
        vec_copy(j, me).start()

    peers(send_parts)

    def factor_copy(slot, i, other):
        return to_rank(factors.at[slot], factors.at[slot], fac_send.at[i], fac_recv.at[i], other)

    factor_copy(k, 0, near).start()
    factor_copy(k, 1, far).start()

    def own_part():
        part_buf[me] = part_src[me]

    only(owners, me, own_part)

    def reduce_parts():
        peers(lambda j: part_copy(j, j).wait_recv())
        total = part_buf[0].astype(F32)
        for j in range(1, n):
            total = total + part_buf[j].astype(F32)
        cross[k, me] = total.astype(BF16)

    only(owners, me, reduce_parts)

    def cross_copy(j, slot):
        return to_peer(cross.at[k, slot], cross.at[k, slot], cross_send.at[j], cross_recv.at[slot], j)

    def rank_copy(slot, i, other, j):
        return to_rank(
            cross.at[slot, j], cross.at[slot, j], rank_send.at[i, j], rank_recv.at[i, j], other
        )

    def pass_on(j):
        rank_copy(k, 1, far, j).start()
        rank_copy(k, 0, near, j).start()

    def send_cross():
        peers(lambda j: cross_copy(j, me).start())
        pass_on(me)

    only(owners, me, send_cross)

    peers(lambda j: vec_copy(j, j).wait_recv())
    vec = vec_buf[0]
    for j in range(1, n):
        vec = vec + vec_buf[j]
    slot_row = lax.broadcasted_iota(jnp.int32, (8, LANES), 0)
    vecs[k] = jnp.where(slot_row == 4, jnp.broadcast_to(g_ref[...], (8, LANES)), vec)

    def vecs_copy(slot, i, other):
        return to_rank(vecs.at[slot], vecs.at[slot], vr_send.at[i], vr_recv.at[i], other)

    for i, other in enumerate((near, far, across)):
        vecs_copy(k, i, other).start()

    def arrived(j):
        cross_copy(j, j).wait_recv()
        pass_on(j)

    peers(lambda j: only(owners, j, lambda: arrived(j)))
    factor_copy(far, 1, far).wait_recv()
    factor_copy(far, 2, near).start()

    def mate_copy(i, src, dst):
        return to_peer(src, dst, mate_send.at[i], mate_recv.at[i], mate)

    expr_copy = mate_copy(0, expr_ref, mate_expr)
    kern_copy = mate_copy(1, krt.at[1 - half], mate_kern)
    u_copy = mate_copy(2, u_buf.at[0], u_buf.at[1])
    expr_copy.start()

    def gradients(kk):
        info = vecs[kk]
        xq_vec, cq_vec, yr_vec, cr_vec, g = (info[i : i + 1] for i in range(5))
        scale = SCALE / g
        dim = x.shape[1]
        cross_xq = cross[kk, :, 0].reshape(dim, LANES)
        cross_yr = cross[kk, :, 1].reshape(dim, LANES)
        grad_q = (norms_one * cr_vec + yr_vec - 2.0 * dot(x, cross_yr)) * scale
        grad_r = (norms_two * cq_vec + xq_vec - 2.0 * dot(y, cross_xq)) * scale
        grads_q[kk] = grad_q
        grads_r[kk] = grad_r
        inner = jnp.sum(cross_xq.astype(F32) * cross_yr.astype(F32), axis=0, keepdims=True)
        curvature = SCALE * (xq_vec * cr_vec + cq_vec * yr_vec - 2.0 * inner)
        grad_g = -curvature / jnp.square(g)
        grads_g[kk] = jnp.broadcast_to(grad_g, (8, LANES))
        return jnp.maximum(
            jnp.max(jnp.maximum(jnp.abs(grad_q), jnp.abs(grad_r)), axis=0, keepdims=True),
            jnp.abs(grad_g),
        )

    peak = gradients(k)
    vecs_copy(near, 0, near).wait_recv()
    each(0, owners, lambda j: rank_copy(near, 0, near, j).wait_recv())
    peak = jnp.maximum(peak, gradients(near))

    def across_x(j):
        rank_copy(far, 1, far, j).wait_recv()
        rank_copy(far, 2, near, j).start()

    each(0, owners, across_x)
    vecs_copy(far, 1, far).wait_recv()
    peak = jnp.maximum(peak, gradients(far))
    vecs_copy(across, 2, across).wait_recv()
    each(0, owners, lambda j: rank_copy(across, 2, near, j).wait_recv())
    peak = jnp.maximum(peak, gradients(across))
    peaks[me] = jnp.broadcast_to(peak, (8, LANES))

    def peak_copy(j, slot):
        return to_peer(peaks.at[me], peaks.at[slot], peak_send.at[j], peak_recv.at[slot], j)

    peers(lambda j: peak_copy(j, me).start())
    factor_copy(near, 0, near).wait_recv()
    factor_copy(across, 2, near).wait_recv()
    log_a, log_b = jnp.log(a_ref[...]), jnp.log(b_ref[...])
    peers(lambda j: peak_copy(j, j).wait_recv())
    top = peaks[0]
    for j in range(1, n):
        top = jnp.maximum(top, peaks[j])
    eta = GAMMA / (jnp.max(top, axis=1, keepdims=True)[0:1] + 1e-6)

    log_g = []
    for kk in range(ranks):
        columns = slice(kk * LANES, (kk + 1) * LANES)
        kern_q = factors[kk, 0].astype(F32) * jnp.exp(-eta * grads_q[kk])
        kern_r = factors[kk, 1].astype(F32) * jnp.exp(-eta * grads_r[kk])
        kq[:, columns] = kern_q.astype(BF16)
        kr[:, columns] = kern_r.astype(BF16)
        kqt[columns, :] = jnp.transpose(kern_q).astype(BF16)
        rows = slice(kk % 2 * LANES, (kk % 2 + 1) * LANES)
        krt[kk // 2, rows, :] = jnp.transpose(kern_r).astype(BF16)
        log_g.append(jnp.log(vecs[kk][4:5]) - eta * grads_g[kk][0:1])
    kern_copy.start()
    log_kern_g = jnp.concatenate(log_g + log_g, axis=0)

    def t_copy(parity, j, slot):
        return to_peer(
            t_buf.at[parity, me], t_buf.at[parity, slot],
            t_send.at[parity, j], t_recv.at[parity, slot], j,
        )

    def whole_krt():
        return krt[...].reshape(ranks * LANES, krt.shape[2])

    def marginals(v):
        s_r = row_product(wide(v, ranks, ranks), whole_krt())
        u_r = jnp.exp(POWER * (log_b - jnp.log(s_r)))
        s_q = row_product(wide(v, 0, ranks), kqt[...])
        u_q = jnp.exp(POWER * (log_a - jnp.log(s_q)))
        return u_q, u_r

    def send_t(parity, u_q, u_r):
        t_buf[parity, me] = tall(row_product(u_q, kq[...]), row_product(u_r, kr[...]))
        peers(lambda j: t_copy(parity, j, me).start())

    def new_weights(parity, v):
        peers(lambda j: t_copy(parity, j, j).wait_recv())
        t = t_buf[parity, 0]
        for j in range(1, n):
            t = t + t_buf[parity, j]
        peers(lambda j: t_copy(parity, j, j).wait_send())
        logs = jnp.log(v * t)
        other = jnp.concatenate([logs[ranks:], logs[:ranks]], axis=0)
        weights = jnp.exp((log_kern_g + logs + other) / 3.0)
        return weights / t, weights, t

    def one_pass(step, v):
        parity = lax.rem(step, 2)
        send_t(parity, *marginals(v))
        return new_weights(parity, v)[0]

    v = lax.fori_loop(0, PASSES - 1, one_pass, jnp.ones((2 * ranks, LANES), F32))
    u_q, u_r = marginals(v)
    u_buf[0] = u_r
    u_copy.start()
    send_t((PASSES - 1) % 2, u_q, u_r)

    share = prof_src.shape[1]

    def prof_copy(line, slot):
        return to_peer(
            prof_src.at[lax.rem(line, tiles)], prof_buf.at[slot],
            prof_send.at[line], prof_recv.at[slot], 2 * line + half,
        )

    left = (krt[half].astype(F32) * u_r).astype(BF16)
    total = dot(left, expr_ref[...])
    expr_copy.wait_recv()
    kern_copy.wait_recv()
    u_copy.wait_recv()
    left = (mate_kern[...].astype(F32) * u_buf[1]).astype(BF16)
    total = total + dot(left, mate_expr[...])
    prof_src[...] = total.astype(BF16).reshape(prof_src.shape)
    lines(lambda line: only(tiles, line, lambda: prof_copy(line, group).start(), groups))

    def own_prof():
        prof_buf[group] = prof_src[group]

    only(tiles, group, own_prof, groups)

    v, weights, t = new_weights((PASSES - 1) % 2, v)
    w_out[...] = pick_row(weights, k) / cells_total
    own_q = q_ref[...] * jnp.exp(-eta * grads_q[k])
    own_r = r_ref[...] * jnp.exp(-eta * grads_r[k])
    q_out[...] = as_column(u_q) * own_q * pick_row(v, k)
    r_out[...] = as_column(u_r) * own_r * pick_row(v, k + ranks)
    stores = [
        pltpu.make_async_copy(src, dst, out_sem.at[i])
        for i, (src, dst) in enumerate(
            (
                (q_out, q_hbm_out), (r_out, r_hbm_out),
                (w_out, w_hbm_out), (pred_out, pred_hbm_out),
            )
        )
    ]
    for store in stores[:3]:
        store.start()
    inverse = as_column(1.0 / row_product(wide(v, 0, ranks), kqt[...]))
    ratio = wide(v[ranks:] / t[:ranks], 0, ranks)
    width = scaled.shape[2]
    for i in range(2):
        columns = slice(i * width, (i + 1) * width)
        scaled[i] = (kq[:, columns].astype(F32) * ratio[:, columns]).astype(BF16)

    def gather_copy(line, slot):
        return to_peer(
            prof.at[half, slot], prof.at[half, slot],
            gat_send.at[line], gat_recv.at[slot], 2 * line + half,
        )

    def forward_copy(side, slot):
        return to_peer(
            prof.at[side, slot], prof.at[side, slot], fwd_send.at[slot], fwd_recv.at[slot], mate
        )

    def reduce_prof():
        lines(lambda line: prof_copy(line, line).wait_recv())
        total = prof_buf[0].astype(F32)
        for line in range(1, groups):
            total = total + prof_buf[line].astype(F32)
        prof[half, group] = total.astype(BF16)
        lines(lambda line: gather_copy(line, group).start())
        forward_copy(half, group).start()

    only(tiles, group, reduce_prof, groups)

    def gathered(line):
        gather_copy(line, line).wait_recv()
        forward_copy(half, line).start()

    lines(lambda line: only(tiles, line, lambda: gathered(line), groups))
    flat = (tiles * share, prof.shape[3])
    mixed = dot(scaled[half], prof[half].reshape(flat))
    each(0, tiles, lambda line: forward_copy(1 - half, line).wait_recv())
    mixed = mixed + dot(scaled[1 - half], prof[1 - half].reshape(flat))
    for i in range(mixed.shape[1] // LANES):
        columns = slice(i * LANES, (i + 1) * LANES)
        pred_out[:, columns] = (mixed[:, columns] * inverse).astype(BF16)

    stores[3].start()

    def sends(j):
        only(owners, j, lambda: part_copy(j, j).wait_send())
        vec_copy(j, j).wait_send()
        only(owners, me, lambda: cross_copy(j, me).wait_send())
        peak_copy(j, j).wait_send()

    peers(sends)

    def line_sends(line):
        only(tiles, line, lambda: prof_copy(line, line).wait_send(), groups)
        only(tiles, group, lambda: gather_copy(line, group).wait_send(), groups)

    lines(line_sends)
    each(0, tiles, lambda line: forward_copy(half, line).wait_send())
    for copy in (expr_copy, kern_copy, u_copy):
        copy.wait_send()
    for i, (slot, other) in enumerate(((k, near), (k, far), (far, near))):
        factor_copy(slot, i, other).wait_send()
        each(0, owners, lambda j: rank_copy(slot, i, other, j).wait_send())
    for i, other in enumerate((near, far, across)):
        vecs_copy(k, i, other).wait_send()
    for store in stores:
        store.wait()


def write_out(*refs):
    count = len(refs) // 2
    sem = refs[-1]
    copies = [
        pltpu.make_async_copy(refs[i], refs[count + i], sem.at[i]) for i in range(count)
    ]
    for copy in copies:
        copy.start()
    for copy in copies:
        copy.wait()


def shards(n, ranks, x_emb, y_emb, q_factor, r_factor, g_weights, a_mass, b_mass, expr):
    rows, dim = x_emb.shape
    genes = expr.shape[1]
    rank_all = ranks * LANES
    owners = min(n, dim // 16)
    groups = n // 2
    tiles = min(groups, rank_all // 2 // 16)
    hbm = pl.BlockSpec(memory_space=pltpu.HBM)
    dma = pltpu.SemaphoreType.DMA
    pair = [dma((n,)), dma((n,))]
    three = [dma((3,)), dma((3,))]
    lined = [dma((groups,)), dma((groups,))]
    block = (rank_all // 2 // tiles, genes)
    shapes = (
        jax.ShapeDtypeStruct(q_factor.shape, F32),
        jax.ShapeDtypeStruct(r_factor.shape, F32),
        jax.ShapeDtypeStruct((1, LANES), F32),
        jax.ShapeDtypeStruct((rows, genes), BF16),
    )
    results = pl.pallas_call(
        functools.partial(kernel, n, ranks, owners, tiles, float(rows * n)),
        out_shape=shapes,
        in_specs=[hbm] * 8,
        out_specs=(hbm,) * 4,
        scratch_shapes=[
            pltpu.VMEM(q_factor.shape, F32),
            pltpu.VMEM(r_factor.shape, F32),
            pltpu.VMEM((1, LANES), F32),
            pltpu.VMEM((rows, genes), BF16),
            dma((4,)),
            pltpu.VMEM(x_emb.shape, BF16),
            pltpu.VMEM(y_emb.shape, BF16),
            pltpu.VMEM(q_factor.shape, F32),
            pltpu.VMEM(r_factor.shape, F32),
            pltpu.VMEM((1, LANES), F32),
            pltpu.VMEM((1, rows), F32),
            pltpu.VMEM((1, rows), F32),
            pltpu.VMEM(expr.shape, BF16),
            dma((8,)),
            pltpu.VMEM((ranks, 2, rows, LANES), BF16),
            pltpu.VMEM((owners, 2, dim // owners, LANES), BF16),
            pltpu.VMEM((n, 2, dim // owners, LANES), BF16),
            pltpu.VMEM((ranks, owners, 2, dim // owners, LANES), BF16),
            pltpu.VMEM((n, 8, LANES), F32),
            pltpu.VMEM((ranks, 8, LANES), F32),
            pltpu.VMEM((ranks, rows, LANES), F32),
            pltpu.VMEM((ranks, rows, LANES), F32),
            pltpu.VMEM((ranks, 8, LANES), F32),
            pltpu.VMEM((n, 8, LANES), F32),
            pltpu.VMEM((rows, rank_all), BF16),
            pltpu.VMEM((rows, rank_all), BF16),
            pltpu.VMEM((rank_all, rows), BF16),
            pltpu.VMEM((2, rank_all // 2, rows), BF16),
            pltpu.VMEM((2, n, 8, LANES), F32),
            pltpu.VMEM((rank_all // 2, rows), BF16),
            pltpu.VMEM(expr.shape, BF16),
            pltpu.VMEM((2, 1, rows), F32),
            pltpu.VMEM((2, rows, rank_all // 2), BF16),
            pltpu.VMEM((tiles,) + block, BF16),
            pltpu.VMEM((groups,) + block, BF16),
            pltpu.VMEM((2, tiles) + block, BF16),
        ]
        + pair + pair + pair + three
        + [dma((3, owners)), dma((3, owners))]
        + three + pair
        + [dma((2, n)), dma((2, n))]
        + three + lined + lined + lined,
        compiler_params=pltpu.CompilerParams(
            collective_id=0, has_side_effects=True, vmem_limit_bytes=VMEM_LIMIT
        ),
        cost_estimate=pl.CostEstimate(
            flops=2 * rows * (2 * dim * LANES + 2 * dim * rank_all + 2 * rank_all * genes),
            bytes_accessed=4 * 1024 * 1024,
            transcendentals=2 * rows * rank_all,
        ),
        name="transport_step",
    )(
        x_emb, y_emb, q_factor, r_factor, g_weights.reshape(1, LANES),
        a_mass.reshape(1, rows), b_mass.reshape(1, rows), expr,
    )
    q_new, r_new, rank_share, predicted = pl.pallas_call(
        write_out,
        out_shape=shapes,
        in_specs=[hbm] * 4,
        out_specs=(hbm,) * 4,
        scratch_shapes=[dma((4,))],
        compiler_params=pltpu.CompilerParams(vmem_limit_bytes=VMEM_LIMIT),
        name="write_out",
    )(*results)
    return q_new, r_new, rank_share.reshape(LANES), predicted


def solution(mesh):
    n, ranks = mesh.shape["cells"], mesh.shape["rank"]
    assert ranks == 4
    return jax.shard_map(
        functools.partial(shards, n, ranks),
        mesh=mesh,
        in_specs=(
            P("cells", None),
            P("cells", None),
            P("cells", "rank"),
            P("cells", "rank"),
            P("rank"),
            P("cells"),
            P("cells"),
            P("cells", "rank"),
        ),
        out_specs=(P("cells", "rank"), P("cells", "rank"), P("rank"), P("cells", "rank")),
        check_vma=False,
    )
```

```python
import functools

import jax
import jax.numpy as jnp
from jax import lax
from jax.experimental import pallas as pl
from jax.experimental.pallas import tpu as pltpu
from jax.sharding import PartitionSpec as P

PASSES = 10
PIECES = 8
SCALE = 0.0625
GAMMA = 10.0
POWER = 0.8
LANES = 128
VMEM_LIMIT = 56 * 1024 * 1024
MESH = pl.DeviceIdType.MESH
F32 = jnp.float32
BF16 = jnp.bfloat16


def dot(left, right):
    return jnp.dot(left, right, preferred_element_type=F32)


def contract_rows(left, right):
    return lax.dot_general(
        left, right, (((0,), (0,)), ((), ())), preferred_element_type=F32
    )


def wide(rows, first, count):
    return jnp.concatenate([rows[first + i : first + i + 1] for i in range(count)], axis=1)


def tall(*rows):
    return jnp.concatenate(
        [row[:, i * LANES : (i + 1) * LANES] for row in rows for i in range(row.shape[1] // LANES)],
        axis=0,
    )


def row_product(row, matrix):
    high = row.astype(BF16).astype(F32)
    low = row - high
    shape = (16, row.shape[1])
    index = lax.broadcasted_iota(jnp.int32, shape, 0)
    parts = jnp.where(
        index == 0,
        jnp.broadcast_to(high, shape),
        jnp.where(index == 1, jnp.broadcast_to(low, shape), 0.0),
    )
    out = dot(parts.astype(BF16), matrix)
    return out[0:1] + out[1:2]


def as_column(row):
    return jnp.transpose(jnp.broadcast_to(row, (LANES, row.shape[1])))


def pick_row(rows, index):
    position = lax.broadcasted_iota(jnp.int32, rows.shape, 0)
    return jnp.sum(jnp.where(position == index, rows, 0.0), axis=0, keepdims=True)


def kernel(
    n, ranks, owners, tiles, cells_total,
    x_hbm, y_hbm, q_hbm, r_hbm, g_hbm, a_hbm, b_hbm, expr_hbm,
    q_hbm_out, r_hbm_out, w_hbm_out, pred_hbm_out,
    q_out, r_out, w_out, pred_out, out_sem,
    x_ref, y_ref, q_ref, r_ref, g_ref, a_ref, b_ref, expr_ref, in_sem,
    factors, part_src, part_buf, cross, vec_buf, vecs, grads_q, grads_r, grads_g,
    peaks, kq, kr, kqt, krt, t_buf, mate_kern, mate_expr, u_buf, scaled,
    prof_src, prof_buf, prof,
    part_send, part_recv, vec_send, vec_recv, cross_send, cross_recv,
    fac_send, fac_recv, rank_send, rank_recv, vr_send, vr_recv,
    peak_send, peak_recv, t_send, t_recv, mate_send, mate_recv,
    prof_send, prof_recv, gat_send, gat_recv, fwd_send, fwd_recv,
):
    me = lax.axis_index("cells")
    k = lax.axis_index("rank")
    near = k + 1 - 2 * lax.rem(k, 2)
    far = lax.rem(k + 2, 4)
    across = 3 - k
    group, half = me // 2, lax.rem(me, 2)
    groups = n // 2
    mate = me + 1 - 2 * half

    def each(first, last, body):
        if last - first <= 8:
            for i in range(first, last):
                body(i)
        else:
            def one(i, carry):
                body(i)
                return carry
            lax.fori_loop(first, last, one, 0)

    def others(index, count):
        if count > 8 or count & (count - 1):
            return lambda body: each(1, count, lambda offset: body(lax.rem(index + offset, count)))
        found = []
        for offset in range(count - 1, 0, -1):
            other = index
            for bit in (1, 2, 4):
                if offset & bit:
                    other = other + bit - 2 * bit * lax.rem(index // bit, 2)
            found.append(other)

        def over(body):
            for other in found:
                body(other)

        return over

    peers = others(me, n)
    lines = others(group, groups)

    def only(limit, index, body, count=n):
        if limit >= count:
            body()
        else:
            pl.when(index < limit)(body)

    def to_peer(src, dst, send, recv, j):
        return pltpu.make_async_remote_copy(
            src_ref=src, dst_ref=dst, send_sem=send, recv_sem=recv,
            device_id=(j, k), device_id_type=MESH,
        )

    def to_rank(src, dst, send, recv, other):
        return pltpu.make_async_remote_copy(
            src_ref=src, dst_ref=dst, send_sem=send, recv_sem=recv,
            device_id=(me, other), device_id_type=MESH,
        )

    loads = [
        pltpu.make_async_copy(src, dst, in_sem.at[i])
        for i, (src, dst) in enumerate(
            (
                (q_hbm, q_ref), (x_hbm, x_ref), (r_hbm, r_ref), (y_hbm, y_ref),
                (g_hbm, g_ref), (a_hbm, a_ref), (b_hbm, b_ref), (expr_hbm, expr_ref),
            )
        )
    ]
    for load in loads:
        load.start()
    barrier = pltpu.get_barrier_semaphore()
    peers(lambda j: pl.semaphore_signal(barrier, inc=1, device_id=(j, k), device_id_type=MESH))
    for other in (near, far, across):
        pl.semaphore_signal(barrier, inc=1, device_id=(me, other), device_id_type=MESH)

    depth = part_src.shape[2]
    loads[0].wait()
    q = q_ref[...]
    q_round = q.astype(BF16)
    factors[k, 0] = q_round
    loads[1].wait()
    x = x_ref[...]
    part_src[:, 0] = contract_rows(x, q_round).astype(BF16).reshape(owners, depth, LANES)
    loads[2].wait()
    r = r_ref[...]
    r_round = r.astype(BF16)
    factors[k, 1] = r_round
    loads[3].wait()
    y = y_ref[...]
    part_src[:, 1] = contract_rows(y, r_round).astype(BF16).reshape(owners, depth, LANES)
    for load in loads[4:]:
        load.wait()
    pl.semaphore_wait(barrier, n - 1 + 3)

    def part_copy(j, slot):
        return to_peer(part_src.at[lax.rem(j, owners)], part_buf.at[slot], part_send.at[j], part_recv.at[slot], j)

    def vec_copy(j, slot):
        return to_peer(vec_buf.at[me], vec_buf.at[slot], vec_send.at[j], vec_recv.at[slot], j)

    peers(lambda j: only(owners, j, lambda: part_copy(j, me).start()))

    def factor_copy(slot, i, other):
        return to_rank(factors.at[slot], factors.at[slot], fac_send.at[i], fac_recv.at[i], other)

    factor_copy(k, 0, near).start()
    factor_copy(k, 1, far).start()

    norms_one = jnp.sum(jnp.square(x.astype(F32)), axis=1, keepdims=True)
    norms_two = jnp.sum(jnp.square(y.astype(F32)), axis=1, keepdims=True)
    vec_buf[me] = jnp.concatenate(
        [
            jnp.sum(norms_one * q, axis=0, keepdims=True),
            jnp.sum(q, axis=0, keepdims=True),
            jnp.sum(norms_two * r, axis=0, keepdims=True),
            jnp.sum(r, axis=0, keepdims=True),
            jnp.zeros((4, LANES), F32),
        ],
        axis=0,
    )
    peers(lambda j: vec_copy(j, me).start())

    def own_part():
        part_buf[me] = part_src[me]

    only(owners, me, own_part)

    def reduce_parts():
        peers(lambda j: part_copy(j, j).wait_recv())
        total = part_buf[0].astype(F32)
        for j in range(1, n):
            total = total + part_buf[j].astype(F32)
        cross[k, me] = total.astype(BF16)

    only(owners, me, reduce_parts)

    def cross_copy(j, slot):
        return to_peer(cross.at[k, slot], cross.at[k, slot], cross_send.at[j], cross_recv.at[slot], j)

    def rank_copy(slot, i, other, j):
        return to_rank(
            cross.at[slot, j], cross.at[slot, j], rank_send.at[i, j], rank_recv.at[i, j], other
        )

    def pass_on(j):
        rank_copy(k, 1, far, j).start()
        rank_copy(k, 0, near, j).start()

    def send_cross():
        peers(lambda j: cross_copy(j, me).start())
        pass_on(me)

    only(owners, me, send_cross)

    peers(lambda j: vec_copy(j, j).wait_recv())
    vec = vec_buf[0]
    for j in range(1, n):
        vec = vec + vec_buf[j]
    slot_row = lax.broadcasted_iota(jnp.int32, (8, LANES), 0)
    vecs[k] = jnp.where(slot_row == 4, jnp.broadcast_to(g_ref[...], (8, LANES)), vec)

    def vecs_copy(slot, i, other):
        return to_rank(vecs.at[slot], vecs.at[slot], vr_send.at[i], vr_recv.at[i], other)

    for i, other in enumerate((near, far, across)):
        vecs_copy(k, i, other).start()

    def arrived(j):
        cross_copy(j, j).wait_recv()
        pass_on(j)

    peers(lambda j: only(owners, j, lambda: arrived(j)))
    factor_copy(far, 1, far).wait_recv()
    factor_copy(far, 2, near).start()

    def expr_copy(piece):
        size = expr_ref.shape[0] // PIECES
        rows = pl.ds(pl.multiple_of(piece * size, size), size)
        return to_peer(
            expr_ref.at[rows], mate_expr.at[rows], mate_send.at[0, piece], mate_recv.at[0, piece], mate
        )

    def kern_copy(piece):
        size = mate_kern.shape[0] // PIECES
        rows = pl.ds(pl.multiple_of(piece * size, size), size)
        return to_peer(
            krt.at[1 - half, rows], mate_kern.at[rows],
            mate_send.at[1, piece], mate_recv.at[1, piece], mate,
        )

    u_copy = to_peer(u_buf.at[0], u_buf.at[1], mate_send.at[2, 0], mate_recv.at[2, 0], mate)

    def gradients(kk):
        info = vecs[kk]
        xq_vec, cq_vec, yr_vec, cr_vec, g = (info[i : i + 1] for i in range(5))
        scale = SCALE / g
        dim = x.shape[1]
        cross_xq = cross[kk, :, 0].reshape(dim, LANES)
        cross_yr = cross[kk, :, 1].reshape(dim, LANES)
        grad_q = (norms_one * cr_vec + yr_vec - 2.0 * dot(x, cross_yr)) * scale
        grad_r = (norms_two * cq_vec + xq_vec - 2.0 * dot(y, cross_xq)) * scale
        grads_q[kk] = grad_q
        grads_r[kk] = grad_r
        inner = jnp.sum(cross_xq.astype(F32) * cross_yr.astype(F32), axis=0, keepdims=True)
        curvature = SCALE * (xq_vec * cr_vec + cq_vec * yr_vec - 2.0 * inner)
        grad_g = -curvature / jnp.square(g)
        grads_g[kk] = jnp.broadcast_to(grad_g, (8, LANES))
        return jnp.maximum(
            jnp.max(jnp.maximum(jnp.abs(grad_q), jnp.abs(grad_r)), axis=0, keepdims=True),
            jnp.abs(grad_g),
        )

    peak = gradients(k)
    vecs_copy(near, 0, near).wait_recv()
    each(0, owners, lambda j: rank_copy(near, 0, near, j).wait_recv())
    peak = jnp.maximum(peak, gradients(near))

    def across_x(j):
        rank_copy(far, 1, far, j).wait_recv()
        rank_copy(far, 2, near, j).start()

    each(0, owners, across_x)
    vecs_copy(far, 1, far).wait_recv()
    peak = jnp.maximum(peak, gradients(far))
    vecs_copy(across, 2, across).wait_recv()
    each(0, owners, lambda j: rank_copy(across, 2, near, j).wait_recv())
    peak = jnp.maximum(peak, gradients(across))
    peaks[me] = jnp.broadcast_to(peak, (8, LANES))

    def peak_copy(j, slot):
        return to_peer(peaks.at[me], peaks.at[slot], peak_send.at[j], peak_recv.at[slot], j)

    peers(lambda j: peak_copy(j, me).start())
    factor_copy(near, 0, near).wait_recv()
    factor_copy(across, 2, near).wait_recv()
    log_a, log_b = jnp.log(a_ref[...]), jnp.log(b_ref[...])
    peers(lambda j: peak_copy(j, j).wait_recv())
    top = peaks[0]
    for j in range(1, n):
        top = jnp.maximum(top, peaks[j])
    eta = GAMMA / (jnp.max(top, axis=1, keepdims=True)[0:1] + 1e-6)

    log_g = []
    for kk in range(ranks):
        columns = slice(kk * LANES, (kk + 1) * LANES)
        kern_q = factors[kk, 0].astype(F32) * jnp.exp(-eta * grads_q[kk])
        kern_r = factors[kk, 1].astype(F32) * jnp.exp(-eta * grads_r[kk])
        kern_q, kern_r = kern_q.astype(BF16), kern_r.astype(BF16)
        kq[:, columns] = kern_q
        kr[:, columns] = kern_r
        kqt[columns, :] = jnp.transpose(kern_q)
        rows = slice(kk % 2 * LANES, (kk % 2 + 1) * LANES)
        krt[kk // 2, rows, :] = jnp.transpose(kern_r)
        log_g.append(jnp.log(vecs[kk][4:5]) - eta * grads_g[kk][0:1])
    log_kern_g = jnp.concatenate(log_g + log_g, axis=0)

    def t_copy(parity, j, slot):
        return to_peer(
            t_buf.at[parity, me], t_buf.at[parity, slot],
            t_send.at[parity, j], t_recv.at[parity, slot], j,
        )

    def whole_krt():
        return krt[...].reshape(ranks * LANES, krt.shape[2])

    def marginals(v):
        s_r = row_product(wide(v, ranks, ranks), whole_krt())
        u_r = jnp.exp(POWER * (log_b - jnp.log(s_r)))
        s_q = row_product(wide(v, 0, ranks), kqt[...])
        u_q = jnp.exp(POWER * (log_a - jnp.log(s_q)))
        return u_q, u_r

    def send_t(parity, u_q, u_r):
        t_buf[parity, me] = tall(row_product(u_q, kq[...]), row_product(u_r, kr[...]))
        peers(lambda j: t_copy(parity, j, me).start())

    def new_weights(parity, v):
        peers(lambda j: t_copy(parity, j, j).wait_recv())
        t = t_buf[parity, 0]
        for j in range(1, n):
            t = t + t_buf[parity, j]
        peers(lambda j: t_copy(parity, j, j).wait_send())
        logs = jnp.log(v * t)
        other = jnp.concatenate([logs[ranks:], logs[:ranks]], axis=0)
        weights = jnp.exp((log_kern_g + logs + other) / 3.0)
        return weights / t, weights, t

    def one_pass(step, v):
        parity = lax.rem(step, 2)
        send_t(parity, *marginals(v))

        @pl.when(step < PIECES)
        def send_piece():
            expr_copy(step).start()
            kern_copy(step).start()

        return new_weights(parity, v)[0]

    v = lax.fori_loop(0, PASSES - 1, one_pass, jnp.ones((2 * ranks, LANES), F32))
    u_q, u_r = marginals(v)
    u_buf[0] = u_r
    u_copy.start()
    send_t((PASSES - 1) % 2, u_q, u_r)

    share = prof_src.shape[1]

    def prof_copy(line, slot):
        return to_peer(
            prof_src.at[lax.rem(line, tiles)], prof_buf.at[slot],
            prof_send.at[line], prof_recv.at[slot], 2 * line + half,
        )

    left = (krt[half].astype(F32) * u_r).astype(BF16)
    total = dot(left, expr_ref[...])
    for piece in range(PIECES):
        expr_copy(piece).wait_recv()
        kern_copy(piece).wait_recv()
    u_copy.wait_recv()
    left = (mate_kern[...].astype(F32) * u_buf[1]).astype(BF16)
    total = total + dot(left, mate_expr[...])
    prof_src[...] = total.astype(BF16).reshape(prof_src.shape)
    lines(lambda line: only(tiles, line, lambda: prof_copy(line, group).start(), groups))

    def own_prof():
        prof_buf[group] = prof_src[group]

    only(tiles, group, own_prof, groups)

    v, weights, t = new_weights((PASSES - 1) % 2, v)
    w_out[...] = pick_row(weights, k) / cells_total
    own_q = q_ref[...] * jnp.exp(-eta * grads_q[k])
    own_r = r_ref[...] * jnp.exp(-eta * grads_r[k])
    q_out[...] = as_column(u_q) * own_q * pick_row(v, k)
    r_out[...] = as_column(u_r) * own_r * pick_row(v, k + ranks)
    stores = [
        pltpu.make_async_copy(src, dst, out_sem.at[i])
        for i, (src, dst) in enumerate(
            (
                (q_out, q_hbm_out), (r_out, r_hbm_out),
                (w_out, w_hbm_out), (pred_out, pred_hbm_out),
            )
        )
    ]
    for store in stores[:3]:
        store.start()
    inverse = as_column(1.0 / row_product(wide(v, 0, ranks), kqt[...]))
    ratio = wide(v[ranks:] / t[:ranks], 0, ranks)
    width = scaled.shape[2]
    for i in range(2):
        columns = slice(i * width, (i + 1) * width)
        scaled[i] = (kq[:, columns].astype(F32) * ratio[:, columns]).astype(BF16)

    def gather_copy(line, slot):
        return to_peer(
            prof.at[half, slot], prof.at[half, slot],
            gat_send.at[line], gat_recv.at[slot], 2 * line + half,
        )

    def forward_copy(side, slot):
        return to_peer(
            prof.at[side, slot], prof.at[side, slot], fwd_send.at[slot], fwd_recv.at[slot], mate
        )

    def reduce_prof():
        lines(lambda line: prof_copy(line, line).wait_recv())
        total = prof_buf[0].astype(F32)
        for line in range(1, groups):
            total = total + prof_buf[line].astype(F32)
        prof[half, group] = total.astype(BF16)
        lines(lambda line: gather_copy(line, group).start())
        forward_copy(half, group).start()

    only(tiles, group, reduce_prof, groups)

    def gathered(line):
        gather_copy(line, line).wait_recv()
        forward_copy(half, line).start()

    lines(lambda line: only(tiles, line, lambda: gathered(line), groups))
    flat = (tiles * share, prof.shape[3])
    mixed = dot(scaled[half], prof[half].reshape(flat))
    each(0, tiles, lambda line: forward_copy(1 - half, line).wait_recv())
    mixed = mixed + dot(scaled[1 - half], prof[1 - half].reshape(flat))
    for i in range(mixed.shape[1] // LANES):
        columns = slice(i * LANES, (i + 1) * LANES)
        pred_out[:, columns] = (mixed[:, columns] * inverse).astype(BF16)

    stores[3].start()

    def sends(j):
        only(owners, j, lambda: part_copy(j, j).wait_send())
        vec_copy(j, j).wait_send()
        only(owners, me, lambda: cross_copy(j, me).wait_send())
        peak_copy(j, j).wait_send()

    peers(sends)

    def line_sends(line):
        only(tiles, line, lambda: prof_copy(line, line).wait_send(), groups)
        only(tiles, group, lambda: gather_copy(line, group).wait_send(), groups)

    lines(line_sends)
    each(0, tiles, lambda line: forward_copy(half, line).wait_send())
    u_copy.wait_send()
    for piece in range(PIECES):
        expr_copy(piece).wait_send()
        kern_copy(piece).wait_send()
    for i, (slot, other) in enumerate(((k, near), (k, far), (far, near))):
        factor_copy(slot, i, other).wait_send()
        each(0, owners, lambda j: rank_copy(slot, i, other, j).wait_send())
    for i, other in enumerate((near, far, across)):
        vecs_copy(k, i, other).wait_send()
    for store in stores:
        store.wait()


def write_out(count, *refs):
    sources, results, held = (refs[i * count : (i + 1) * count] for i in range(3))
    load_sem, store_sem = refs[3 * count :]
    loads = [
        pltpu.make_async_copy(sources[i], held[i], load_sem.at[i]) for i in range(count)
    ]
    stores = [
        pltpu.make_async_copy(held[i], results[i], store_sem.at[i]) for i in range(count)
    ]
    for load in loads:
        load.start()
    for load, store in zip(loads, stores):
        load.wait()
        store.start()
    for store in stores:
        store.wait()


def shards(n, ranks, x_emb, y_emb, q_factor, r_factor, g_weights, a_mass, b_mass, expr):
    rows, dim = x_emb.shape
    genes = expr.shape[1]
    rank_all = ranks * LANES
    owners = min(n, dim // 16)
    groups = n // 2
    tiles = min(groups, rank_all // 2 // 16)
    hbm = pl.BlockSpec(memory_space=pltpu.HBM)
    dma = pltpu.SemaphoreType.DMA
    pair = [dma((n,)), dma((n,))]
    three = [dma((3,)), dma((3,))]
    lined = [dma((groups,)), dma((groups,))]
    block = (rank_all // 2 // tiles, genes)
    shapes = (
        jax.ShapeDtypeStruct(q_factor.shape, F32),
        jax.ShapeDtypeStruct(r_factor.shape, F32),
        jax.ShapeDtypeStruct((1, LANES), F32),
        jax.ShapeDtypeStruct((rows, genes), BF16),
    )
    results = pl.pallas_call(
        functools.partial(kernel, n, ranks, owners, tiles, float(rows * n)),
        out_shape=shapes,
        in_specs=[hbm] * 8,
        out_specs=(hbm,) * 4,
        scratch_shapes=[
            pltpu.VMEM(q_factor.shape, F32),
            pltpu.VMEM(r_factor.shape, F32),
            pltpu.VMEM((1, LANES), F32),
            pltpu.VMEM((rows, genes), BF16),
            dma((4,)),
            pltpu.VMEM(x_emb.shape, BF16),
            pltpu.VMEM(y_emb.shape, BF16),
            pltpu.VMEM(q_factor.shape, F32),
            pltpu.VMEM(r_factor.shape, F32),
            pltpu.VMEM((1, LANES), F32),
            pltpu.VMEM((1, rows), F32),
            pltpu.VMEM((1, rows), F32),
            pltpu.VMEM(expr.shape, BF16),
            dma((8,)),
            pltpu.VMEM((ranks, 2, rows, LANES), BF16),
            pltpu.VMEM((owners, 2, dim // owners, LANES), BF16),
            pltpu.VMEM((n, 2, dim // owners, LANES), BF16),
            pltpu.VMEM((ranks, owners, 2, dim // owners, LANES), BF16),
            pltpu.VMEM((n, 8, LANES), F32),
            pltpu.VMEM((ranks, 8, LANES), F32),
            pltpu.VMEM((ranks, rows, LANES), F32),
            pltpu.VMEM((ranks, rows, LANES), F32),
            pltpu.VMEM((ranks, 8, LANES), F32),
            pltpu.VMEM((n, 8, LANES), F32),
            pltpu.VMEM((rows, rank_all), BF16),
            pltpu.VMEM((rows, rank_all), BF16),
            pltpu.VMEM((rank_all, rows), BF16),
            pltpu.VMEM((2, rank_all // 2, rows), BF16),
            pltpu.VMEM((2, n, 8, LANES), F32),
            pltpu.VMEM((rank_all // 2, rows), BF16),
            pltpu.VMEM(expr.shape, BF16),
            pltpu.VMEM((2, 1, rows), F32),
            pltpu.VMEM((2, rows, rank_all // 2), BF16),
            pltpu.VMEM((tiles,) + block, BF16),
            pltpu.VMEM((groups,) + block, BF16),
            pltpu.VMEM((2, tiles) + block, BF16),
        ]
        + pair + pair + pair + three
        + [dma((3, owners)), dma((3, owners))]
        + three + pair
        + [dma((2, n)), dma((2, n))]
        + [dma((3, PIECES)), dma((3, PIECES))]
        + lined + lined + lined,
        compiler_params=pltpu.CompilerParams(
            collective_id=0, has_side_effects=True, vmem_limit_bytes=VMEM_LIMIT
        ),
        cost_estimate=pl.CostEstimate(
            flops=2 * rows * (2 * dim * LANES + 2 * dim * rank_all + 2 * rank_all * genes),
            bytes_accessed=4 * 1024 * 1024,
            transcendentals=2 * rows * rank_all,
        ),
        name="transport_step",
    )(
        x_emb, y_emb, q_factor, r_factor, g_weights.reshape(1, LANES),
        a_mass.reshape(1, rows), b_mass.reshape(1, rows), expr,
    )
    q_new, r_new, rank_share, predicted = pl.pallas_call(
        functools.partial(write_out, len(shapes)),
        out_shape=shapes,
        in_specs=[hbm] * 4,
        out_specs=(hbm,) * 4,
        scratch_shapes=[pltpu.VMEM(shape.shape, shape.dtype) for shape in shapes]
        + [dma((len(shapes),)), dma((len(shapes),))],
        compiler_params=pltpu.CompilerParams(vmem_limit_bytes=VMEM_LIMIT),
        name="write_out",
    )(*results)
    return q_new, r_new, rank_share.reshape(LANES), predicted


def solution(mesh):
    n, ranks = mesh.shape["cells"], mesh.shape["rank"]
    assert ranks == 4
    return jax.shard_map(
        functools.partial(shards, n, ranks),
        mesh=mesh,
        in_specs=(
            P("cells", None),
            P("cells", None),
            P("cells", "rank"),
            P("cells", "rank"),
            P("rank"),
            P("cells"),
            P("cells"),
            P("cells", "rank"),
        ),
        out_specs=(P("cells", "rank"), P("cells", "rank"), P("rank"), P("cells", "rank")),
        check_vma=False,
    )
```

```python
import functools

import jax
import jax.numpy as jnp
from jax import lax
from jax.experimental import pallas as pl
from jax.experimental.pallas import tpu as pltpu
from jax.sharding import PartitionSpec as P

PASSES = 10
PIECES = 8
BLOCKS = 4
SCALE = 0.0625
GAMMA = 10.0
POWER = 0.8
LANES = 128
VMEM_LIMIT = 56 * 1024 * 1024
MESH = pl.DeviceIdType.MESH
F32 = jnp.float32
BF16 = jnp.bfloat16


def dot(left, right):
    return jnp.dot(left, right, preferred_element_type=F32)


def contract_rows(left, right):
    return lax.dot_general(
        left, right, (((0,), (0,)), ((), ())), preferred_element_type=F32
    )


def wide(rows, first, count):
    return jnp.concatenate([rows[first + i : first + i + 1] for i in range(count)], axis=1)


def tall(*rows):
    return jnp.concatenate(
        [row[:, i * LANES : (i + 1) * LANES] for row in rows for i in range(row.shape[1] // LANES)],
        axis=0,
    )


def row_product(row, matrix):
    high = row.astype(BF16).astype(F32)
    low = row - high
    shape = (16, row.shape[1])
    index = lax.broadcasted_iota(jnp.int32, shape, 0)
    parts = jnp.where(
        index == 0,
        jnp.broadcast_to(high, shape),
        jnp.where(index == 1, jnp.broadcast_to(low, shape), 0.0),
    )
    out = dot(parts.astype(BF16), matrix)
    return out[0:1] + out[1:2]


def as_column(row):
    return jnp.transpose(jnp.broadcast_to(row, (LANES, row.shape[1])))


def pick_row(rows, index):
    position = lax.broadcasted_iota(jnp.int32, rows.shape, 0)
    return jnp.sum(jnp.where(position == index, rows, 0.0), axis=0, keepdims=True)


def kernel(
    n, ranks, owners, tiles, cells_total,
    x_hbm, y_hbm, q_hbm, r_hbm, g_hbm, a_hbm, b_hbm, expr_hbm,
    q_hbm_out, r_hbm_out, w_hbm_out, pred_hbm_out,
    q_out, r_out, w_out, pred_out, out_sem,
    x_ref, y_ref, q_ref, r_ref, g_ref, a_ref, b_ref, expr_ref, in_sem,
    factors, part_src, part_buf, cross, vec_buf, vecs, grads_q, grads_r, grads_g,
    peaks, kq, kr, kqt, krt, t_buf, mate_kern, mate_expr, u_buf, scaled,
    prof_src, prof_buf, prof,
    part_send, part_recv, vec_send, vec_recv, cross_send, cross_recv,
    fac_send, fac_recv, rank_send, rank_recv, vr_send, vr_recv,
    peak_send, peak_recv, t_send, t_recv, mate_send, mate_recv,
    prof_send, prof_recv, gat_send, gat_recv, fwd_send, fwd_recv,
):
    me = lax.axis_index("cells")
    k = lax.axis_index("rank")
    near = k + 1 - 2 * lax.rem(k, 2)
    far = lax.rem(k + 2, 4)
    across = 3 - k
    group, half = me // 2, lax.rem(me, 2)
    groups = n // 2
    mate = me + 1 - 2 * half

    def each(first, last, body):
        if last - first <= 8:
            for i in range(first, last):
                body(i)
        else:
            def one(i, carry):
                body(i)
                return carry
            lax.fori_loop(first, last, one, 0)

    def others(index, count):
        if count > 8 or count & (count - 1):
            return lambda body, reverse=False: each(
                1, count, lambda offset: body(lax.rem(index + offset, count))
            )
        found = []
        for offset in range(count - 1, 0, -1):
            other = index
            for bit in (1, 2, 4):
                if offset & bit:
                    other = other + bit - 2 * bit * lax.rem(index // bit, 2)
            found.append(other)

        def over(body, reverse=False):
            for other in found[::-1] if reverse else found:
                body(other)

        return over

    peers = others(me, n)
    lines = others(group, groups)

    def only(limit, index, body, count=n):
        if limit >= count:
            body()
        else:
            pl.when(index < limit)(body)

    def to_peer(src, dst, send, recv, j):
        return pltpu.make_async_remote_copy(
            src_ref=src, dst_ref=dst, send_sem=send, recv_sem=recv,
            device_id=(j, k), device_id_type=MESH,
        )

    def to_rank(src, dst, send, recv, other):
        return pltpu.make_async_remote_copy(
            src_ref=src, dst_ref=dst, send_sem=send, recv_sem=recv,
            device_id=(me, other), device_id_type=MESH,
        )

    def all_copies(slots, send, recv):
        most = slots.at[pl.ds(0, n - 1)]
        return to_peer(most, most, send, recv, mate)

    loads = [
        pltpu.make_async_copy(src, dst, in_sem.at[i])
        for i, (src, dst) in enumerate(
            (
                (q_hbm, q_ref), (x_hbm, x_ref), (r_hbm, r_ref), (y_hbm, y_ref),
                (g_hbm, g_ref), (a_hbm, a_ref), (b_hbm, b_ref), (expr_hbm, expr_ref),
            )
        )
    ]
    for load in loads:
        load.start()
    barrier = pltpu.get_barrier_semaphore()
    peers(lambda j: pl.semaphore_signal(barrier, inc=1, device_id=(j, k), device_id_type=MESH))
    for other in (near, far, across):
        pl.semaphore_signal(barrier, inc=1, device_id=(me, other), device_id_type=MESH)

    depth = part_src.shape[2]
    loads[0].wait()
    q = q_ref[...]
    q_round = q.astype(BF16)
    factors[k, 0] = q_round
    loads[1].wait()
    x = x_ref[...]
    part_src[:, 0] = contract_rows(x, q_round).astype(BF16).reshape(owners, depth, LANES)
    loads[2].wait()
    r = r_ref[...]
    r_round = r.astype(BF16)
    factors[k, 1] = r_round
    loads[3].wait()
    y = y_ref[...]
    part_src[:, 1] = contract_rows(y, r_round).astype(BF16).reshape(owners, depth, LANES)
    for load in loads[4:]:
        load.wait()
    pl.semaphore_wait(barrier, n - 1 + 3)

    def part_copy(j, slot):
        return to_peer(part_src.at[lax.rem(j, owners)], part_buf.at[slot], part_send.at[j], part_recv.at[slot], j)

    def vec_copy(j, slot):
        return to_peer(vec_buf.at[me], vec_buf.at[slot], vec_send.at[0], vec_recv.at[0], j)

    peers(lambda j: only(owners, j, lambda: part_copy(j, me).start()))

    def factor_copy(slot, i, other):
        return to_rank(factors.at[slot], factors.at[slot], fac_send.at[i], fac_recv.at[i], other)

    factor_copy(k, 0, near).start()
    factor_copy(k, 1, far).start()

    norms_one = jnp.sum(jnp.square(x.astype(F32)), axis=1, keepdims=True)
    norms_two = jnp.sum(jnp.square(y.astype(F32)), axis=1, keepdims=True)
    vec_buf[me] = jnp.concatenate(
        [
            jnp.sum(norms_one * q, axis=0, keepdims=True),
            jnp.sum(q, axis=0, keepdims=True),
            jnp.sum(norms_two * r, axis=0, keepdims=True),
            jnp.sum(r, axis=0, keepdims=True),
            jnp.zeros((4, LANES), F32),
        ],
        axis=0,
    )
    peers(lambda j: vec_copy(j, me).start())

    def own_part():
        part_buf[me] = part_src[me]

    only(owners, me, own_part)

    def reduce_parts():
        peers(lambda j: part_copy(j, j).wait_recv())
        total = part_buf[0].astype(F32)
        for j in range(1, n):
            total = total + part_buf[j].astype(F32)
        cross[k, me] = total.astype(BF16)

    only(owners, me, reduce_parts)

    def cross_copy(j, slot):
        return to_peer(cross.at[k, slot], cross.at[k, slot], cross_send.at[j], cross_recv.at[slot], j)

    def rank_copy(slot, i, other, j):
        return to_rank(
            cross.at[slot, j], cross.at[slot, j], rank_send.at[i, j], rank_recv.at[i, j], other
        )

    def pass_on(j):
        rank_copy(k, 1, far, j).start()
        rank_copy(k, 0, near, j).start()

    def send_cross():
        peers(lambda j: cross_copy(j, me).start())
        pass_on(me)

    only(owners, me, send_cross)

    all_copies(vec_buf, vec_send.at[0], vec_recv.at[0]).wait_recv()
    vec = vec_buf[0]
    for j in range(1, n):
        vec = vec + vec_buf[j]
    slot_row = lax.broadcasted_iota(jnp.int32, (8, LANES), 0)
    vecs[k] = jnp.where(slot_row == 4, jnp.broadcast_to(g_ref[...], (8, LANES)), vec)

    def vecs_copy(slot, i, other):
        return to_rank(vecs.at[slot], vecs.at[slot], vr_send.at[i], vr_recv.at[i], other)

    for i, other in enumerate((near, far, across)):
        vecs_copy(k, i, other).start()

    def arrived(j):
        cross_copy(j, j).wait_recv()
        pass_on(j)

    peers(lambda j: only(owners, j, lambda: arrived(j)), reverse=True)
    factor_copy(far, 1, far).wait_recv()
    factor_copy(far, 2, near).start()

    def expr_copy(piece):
        size = expr_ref.shape[0] // PIECES
        rows = pl.ds(pl.multiple_of(piece * size, size), size)
        return to_peer(
            expr_ref.at[rows], mate_expr.at[rows], mate_send.at[0, piece], mate_recv.at[0, piece], mate
        )

    def kern_copy(piece):
        size = mate_kern.shape[0] // PIECES
        rows = pl.ds(pl.multiple_of(piece * size, size), size)
        return to_peer(
            krt.at[1 - half, rows], mate_kern.at[rows],
            mate_send.at[1, piece], mate_recv.at[1, piece], mate,
        )

    u_copy = to_peer(u_buf.at[0], u_buf.at[1], mate_send.at[2, 0], mate_recv.at[2, 0], mate)

    def gradients(kk):
        info = vecs[kk]
        xq_vec, cq_vec, yr_vec, cr_vec, g = (info[i : i + 1] for i in range(5))
        scale = SCALE / g
        dim = x.shape[1]
        cross_xq = cross[kk, :, 0].reshape(dim, LANES)
        cross_yr = cross[kk, :, 1].reshape(dim, LANES)
        grad_q = (norms_one * cr_vec + yr_vec - 2.0 * dot(x, cross_yr)) * scale
        grad_r = (norms_two * cq_vec + xq_vec - 2.0 * dot(y, cross_xq)) * scale
        grads_q[kk] = grad_q
        grads_r[kk] = grad_r
        inner = jnp.sum(cross_xq.astype(F32) * cross_yr.astype(F32), axis=0, keepdims=True)
        curvature = SCALE * (xq_vec * cr_vec + cq_vec * yr_vec - 2.0 * inner)
        grad_g = -curvature / jnp.square(g)
        grads_g[kk] = jnp.broadcast_to(grad_g, (8, LANES))
        return jnp.maximum(
            jnp.max(jnp.maximum(jnp.abs(grad_q), jnp.abs(grad_r)), axis=0, keepdims=True),
            jnp.abs(grad_g),
        )

    peak = gradients(k)
    vecs_copy(near, 0, near).wait_recv()
    each(0, owners, lambda j: rank_copy(near, 0, near, j).wait_recv())
    peak = jnp.maximum(peak, gradients(near))

    def across_x(j):
        rank_copy(far, 1, far, j).wait_recv()
        rank_copy(far, 2, near, j).start()

    each(0, owners, across_x)
    vecs_copy(far, 1, far).wait_recv()
    peak = jnp.maximum(peak, gradients(far))
    vecs_copy(across, 2, across).wait_recv()
    each(0, owners, lambda j: rank_copy(across, 2, near, j).wait_recv())
    peak = jnp.maximum(peak, gradients(across))
    peaks[me] = jnp.broadcast_to(peak, (8, LANES))

    def peak_copy(j, slot):
        return to_peer(peaks.at[me], peaks.at[slot], peak_send.at[0], peak_recv.at[0], j)

    peers(lambda j: peak_copy(j, me).start())
    factor_copy(near, 0, near).wait_recv()
    factor_copy(across, 2, near).wait_recv()
    log_a, log_b = jnp.log(a_ref[...]), jnp.log(b_ref[...])
    all_copies(peaks, peak_send.at[0], peak_recv.at[0]).wait_recv()
    top = peaks[0]
    for j in range(1, n):
        top = jnp.maximum(top, peaks[j])
    eta = GAMMA / (jnp.max(top, axis=1, keepdims=True)[0:1] + 1e-6)

    log_g = []
    for kk in range(ranks):
        columns = slice(kk * LANES, (kk + 1) * LANES)
        kern_q = factors[kk, 0].astype(F32) * jnp.exp(-eta * grads_q[kk])
        kern_r = factors[kk, 1].astype(F32) * jnp.exp(-eta * grads_r[kk])
        kern_q, kern_r = kern_q.astype(BF16), kern_r.astype(BF16)
        kq[:, columns] = kern_q
        kr[:, columns] = kern_r
        kqt[columns, :] = jnp.transpose(kern_q)
        rows = slice(kk % 2 * LANES, (kk % 2 + 1) * LANES)
        krt[kk // 2, rows, :] = jnp.transpose(kern_r)
        log_g.append(jnp.log(vecs[kk][4:5]) - eta * grads_g[kk][0:1])
    log_kern_g = jnp.concatenate(log_g + log_g, axis=0)

    def t_copy(parity, j, slot):
        return to_peer(
            t_buf.at[parity, me], t_buf.at[parity, slot],
            t_send.at[parity], t_recv.at[parity], j,
        )

    def t_all(parity):
        return all_copies(t_buf.at[parity], t_send.at[parity], t_recv.at[parity])

    def whole_krt():
        return krt[...].reshape(ranks * LANES, krt.shape[2])

    def marginals(v):
        s_r = row_product(wide(v, ranks, ranks), whole_krt())
        u_r = jnp.exp(POWER * (log_b - jnp.log(s_r)))
        s_q = row_product(wide(v, 0, ranks), kqt[...])
        u_q = jnp.exp(POWER * (log_a - jnp.log(s_q)))
        return u_q, u_r

    def send_t(parity, u_q, u_r):
        t_buf[parity, me] = tall(row_product(u_q, kq[...]), row_product(u_r, kr[...]))
        peers(lambda j: t_copy(parity, j, me).start())

    def new_weights(parity, v):
        t_all(parity).wait_recv()
        t = t_buf[parity, 0]
        for j in range(1, n):
            t = t + t_buf[parity, j]
        t_all(parity).wait_send()
        logs = jnp.log(v * t)
        other = jnp.concatenate([logs[ranks:], logs[:ranks]], axis=0)
        weights = jnp.exp((log_kern_g + logs + other) / 3.0)
        return weights / t, weights, t

    def one_pass(step, v):
        parity = lax.rem(step, 2)
        send_t(parity, *marginals(v))

        @pl.when(step < PIECES)
        def send_piece():
            expr_copy(step).start()
            kern_copy(step).start()

        return new_weights(parity, v)[0]

    v = lax.fori_loop(0, PASSES - 1, one_pass, jnp.ones((2 * ranks, LANES), F32))
    u_q, u_r = marginals(v)
    u_buf[0] = u_r
    u_copy.start()
    send_t((PASSES - 1) % 2, u_q, u_r)

    share = prof_src.shape[1]

    def prof_copy(line, slot):
        return to_peer(
            prof_src.at[lax.rem(line, tiles)], prof_buf.at[slot],
            prof_send.at[line], prof_recv.at[slot], 2 * line + half,
        )

    left = (krt[half].astype(F32) * u_r).astype(BF16)
    total = dot(left, expr_ref[...])
    for piece in range(PIECES):
        expr_copy(piece).wait_recv()
        kern_copy(piece).wait_recv()
    u_copy.wait_recv()
    left = (mate_kern[...].astype(F32) * u_buf[1]).astype(BF16)
    total = total + dot(left, mate_expr[...])
    prof_src[...] = total.astype(BF16).reshape(prof_src.shape)
    lines(lambda line: only(tiles, line, lambda: prof_copy(line, group).start(), groups))

    def own_prof():
        prof_buf[group] = prof_src[group]

    only(tiles, group, own_prof, groups)

    v, weights, t = new_weights((PASSES - 1) % 2, v)

    def sends(j):
        only(owners, j, lambda: part_copy(j, j).wait_send())
        only(owners, me, lambda: cross_copy(j, me).wait_send())

    peers(sends)
    all_copies(vec_buf, vec_send.at[0], vec_recv.at[0]).wait_send()
    all_copies(peaks, peak_send.at[0], peak_recv.at[0]).wait_send()
    for i, (slot, other) in enumerate(((k, near), (k, far), (far, near))):
        factor_copy(slot, i, other).wait_send()
        each(0, owners, lambda j: rank_copy(slot, i, other, j).wait_send())
    for i, other in enumerate((near, far, across)):
        vecs_copy(k, i, other).wait_send()
    u_copy.wait_send()
    for piece in range(PIECES):
        expr_copy(piece).wait_send()
        kern_copy(piece).wait_send()
    w_out[...] = pick_row(weights, k) / cells_total
    own_q = q_ref[...] * jnp.exp(-eta * grads_q[k])
    own_r = r_ref[...] * jnp.exp(-eta * grads_r[k])
    q_out[...] = as_column(u_q) * own_q * pick_row(v, k)
    r_out[...] = as_column(u_r) * own_r * pick_row(v, k + ranks)
    def block_rows(i):
        size = pred_out.shape[0] // BLOCKS
        return slice(i * size, (i + 1) * size)

    stores = [
        pltpu.make_async_copy(src, dst, out_sem.at[i])
        for i, (src, dst) in enumerate(
            (
                (q_out, q_hbm_out), (r_out, r_hbm_out),
                (w_out, w_hbm_out),
            )
            + tuple(
                (pred_out.at[block_rows(i)], pred_hbm_out.at[block_rows(i)])
                for i in range(BLOCKS)
            )
        )
    ]
    for store in stores[:3]:
        store.start()
    inverse = as_column(1.0 / row_product(wide(v, 0, ranks), kqt[...]))
    ratio = wide(v[ranks:] / t[:ranks], 0, ranks)
    width = scaled.shape[2]
    for i in range(2):
        columns = slice(i * width, (i + 1) * width)
        scaled[i] = (kq[:, columns].astype(F32) * ratio[:, columns]).astype(BF16)

    def gather_copy(line, slot):
        return to_peer(
            prof.at[half, slot], prof.at[half, slot],
            gat_send.at[line], gat_recv.at[slot], 2 * line + half,
        )

    def forward_copy(side, slot):
        return to_peer(
            prof.at[side, slot], prof.at[side, slot], fwd_send.at[slot], fwd_recv.at[slot], mate
        )

    def reduce_prof():
        lines(lambda line: prof_copy(line, line).wait_recv())
        total = prof_buf[0].astype(F32)
        for line in range(1, groups):
            total = total + prof_buf[line].astype(F32)
        prof[half, group] = total.astype(BF16)
        lines(lambda line: gather_copy(line, group).start())
        forward_copy(half, group).start()

    only(tiles, group, reduce_prof, groups)

    def gathered(line):
        gather_copy(line, line).wait_recv()
        forward_copy(half, line).start()

    lines(lambda line: only(tiles, line, lambda: gathered(line), groups), reverse=True)
    flat = (tiles * share, prof.shape[3])
    each(0, tiles, lambda line: forward_copy(1 - half, line).wait_recv())
    for i in range(BLOCKS):
        rows = block_rows(i)
        mixed = dot(scaled[half, rows], prof[half].reshape(flat))
        mixed = mixed + dot(scaled[1 - half, rows], prof[1 - half].reshape(flat))
        across_genes = jnp.concatenate([inverse[rows]] * (mixed.shape[1] // LANES), axis=1)
        pred_out[rows] = (mixed * across_genes).astype(BF16)
        stores[3 + i].start()

    def last_sends(line):
        only(tiles, group, lambda: gather_copy(line, group).wait_send(), groups)

    lines(last_sends)
    lines(lambda line: only(tiles, line, lambda: prof_copy(line, line).wait_send(), groups))
    each(0, tiles, lambda line: forward_copy(half, line).wait_send())
    for store in stores:
        store.wait()


def write_out(count, *refs):
    sources, results, held = (refs[i * count : (i + 1) * count] for i in range(3))
    load_sem, store_sem = refs[3 * count :]
    loads, stores = [], []
    for source, result, hold in zip(sources, results, held):
        pieces = BLOCKS if source.shape[0] > BLOCKS else 1
        size = source.shape[0] // pieces
        for i in range(pieces):
            rows = pl.ds(i * size, size)
            sem = len(loads)
            loads.append(
                pltpu.make_async_copy(source.at[rows], hold.at[rows], load_sem.at[sem])
            )
            stores.append(
                pltpu.make_async_copy(hold.at[rows], result.at[rows], store_sem.at[sem])
            )
    for load in loads:
        load.start()
    for load, store in zip(loads, stores):
        load.wait()
        store.start()
    for store in stores:
        store.wait()


def shards(n, ranks, x_emb, y_emb, q_factor, r_factor, g_weights, a_mass, b_mass, expr):
    rows, dim = x_emb.shape
    genes = expr.shape[1]
    rank_all = ranks * LANES
    owners = min(n, dim // 16)
    groups = n // 2
    tiles = min(groups, rank_all // 2 // 16)
    hbm = pl.BlockSpec(memory_space=pltpu.HBM)
    dma = pltpu.SemaphoreType.DMA
    pair = [dma((n,)), dma((n,))]
    single = [dma((1,)), dma((1,))]
    three = [dma((3,)), dma((3,))]
    lined = [dma((groups,)), dma((groups,))]
    block = (rank_all // 2 // tiles, genes)
    shapes = (
        jax.ShapeDtypeStruct(q_factor.shape, F32),
        jax.ShapeDtypeStruct(r_factor.shape, F32),
        jax.ShapeDtypeStruct((1, LANES), F32),
        jax.ShapeDtypeStruct((rows, genes), BF16),
    )
    results = pl.pallas_call(
        functools.partial(kernel, n, ranks, owners, tiles, float(rows * n)),
        out_shape=shapes,
        in_specs=[hbm] * 8,
        out_specs=(hbm,) * 4,
        scratch_shapes=[
            pltpu.VMEM(q_factor.shape, F32),
            pltpu.VMEM(r_factor.shape, F32),
            pltpu.VMEM((1, LANES), F32),
            pltpu.VMEM((rows, genes), BF16),
            dma((3 + BLOCKS,)),
            pltpu.VMEM(x_emb.shape, BF16),
            pltpu.VMEM(y_emb.shape, BF16),
            pltpu.VMEM(q_factor.shape, F32),
            pltpu.VMEM(r_factor.shape, F32),
            pltpu.VMEM((1, LANES), F32),
            pltpu.VMEM((1, rows), F32),
            pltpu.VMEM((1, rows), F32),
            pltpu.VMEM(expr.shape, BF16),
            dma((8,)),
            pltpu.VMEM((ranks, 2, rows, LANES), BF16),
            pltpu.VMEM((owners, 2, dim // owners, LANES), BF16),
            pltpu.VMEM((n, 2, dim // owners, LANES), BF16),
            pltpu.VMEM((ranks, owners, 2, dim // owners, LANES), BF16),
            pltpu.VMEM((n, 8, LANES), F32),
            pltpu.VMEM((ranks, 8, LANES), F32),
            pltpu.VMEM((ranks, rows, LANES), F32),
            pltpu.VMEM((ranks, rows, LANES), F32),
            pltpu.VMEM((ranks, 8, LANES), F32),
            pltpu.VMEM((n, 8, LANES), F32),
            pltpu.VMEM((rows, rank_all), BF16),
            pltpu.VMEM((rows, rank_all), BF16),
            pltpu.VMEM((rank_all, rows), BF16),
            pltpu.VMEM((2, rank_all // 2, rows), BF16),
            pltpu.VMEM((2, n, 8, LANES), F32),
            pltpu.VMEM((rank_all // 2, rows), BF16),
            pltpu.VMEM(expr.shape, BF16),
            pltpu.VMEM((2, 1, rows), F32),
            pltpu.VMEM((2, rows, rank_all // 2), BF16),
            pltpu.VMEM((tiles,) + block, BF16),
            pltpu.VMEM((groups,) + block, BF16),
            pltpu.VMEM((2, tiles) + block, BF16),
        ]
        + pair + single + pair + three
        + [dma((3, owners)), dma((3, owners))]
        + three + single
        + [dma((2,)), dma((2,))]
        + [dma((3, PIECES)), dma((3, PIECES))]
        + lined + lined + lined,
        compiler_params=pltpu.CompilerParams(
            collective_id=0, has_side_effects=True, vmem_limit_bytes=VMEM_LIMIT
        ),
        cost_estimate=pl.CostEstimate(
            flops=2 * rows * (2 * dim * LANES + 2 * dim * rank_all + 2 * rank_all * genes),
            bytes_accessed=4 * 1024 * 1024,
            transcendentals=2 * rows * rank_all,
        ),
        name="transport_step",
    )(
        x_emb, y_emb, q_factor, r_factor, g_weights.reshape(1, LANES),
        a_mass.reshape(1, rows), b_mass.reshape(1, rows), expr,
    )
    q_new, r_new, rank_share, predicted = pl.pallas_call(
        functools.partial(write_out, len(shapes)),
        out_shape=shapes,
        in_specs=[hbm] * 4,
        out_specs=(hbm,) * 4,
        scratch_shapes=[pltpu.VMEM(shape.shape, shape.dtype) for shape in shapes]
        + [dma((len(shapes) * BLOCKS,)), dma((len(shapes) * BLOCKS,))],
        compiler_params=pltpu.CompilerParams(vmem_limit_bytes=VMEM_LIMIT),
        name="write_out",
    )(*results)
    return q_new, r_new, rank_share.reshape(LANES), predicted


def solution(mesh):
    n, ranks = mesh.shape["cells"], mesh.shape["rank"]
    assert ranks == 4
    return jax.shard_map(
        functools.partial(shards, n, ranks),
        mesh=mesh,
        in_specs=(
            P("cells", None),
            P("cells", None),
            P("cells", "rank"),
            P("cells", "rank"),
            P("rank"),
            P("cells"),
            P("cells"),
            P("cells", "rank"),
        ),
        out_specs=(P("cells", "rank"), P("cells", "rank"), P("rank"), P("cells", "rank")),
        check_vma=False,
    )
```

```python
import functools

import jax
import jax.numpy as jnp
from jax import lax
from jax.experimental import pallas as pl
from jax.experimental.pallas import tpu as pltpu
from jax.sharding import PartitionSpec as P

PASSES = 10
PIECES = 8
BLOCKS = 4
HALVES = 2
SCALE = 0.0625
GAMMA = 10.0
POWER = 0.8
LANES = 128
VMEM_LIMIT = 56 * 1024 * 1024
MESH = pl.DeviceIdType.MESH
F32 = jnp.float32
BF16 = jnp.bfloat16


def dot(left, right):
    return jnp.dot(left, right, preferred_element_type=F32)


def contract_rows(left, right):
    return lax.dot_general(
        left, right, (((0,), (0,)), ((), ())), preferred_element_type=F32
    )


def wide(rows, first, count):
    return jnp.concatenate([rows[first + i : first + i + 1] for i in range(count)], axis=1)


def tall(*rows):
    return jnp.concatenate(
        [row[:, i * LANES : (i + 1) * LANES] for row in rows for i in range(row.shape[1] // LANES)],
        axis=0,
    )


def row_product(row, matrix):
    high = row.astype(BF16).astype(F32)
    low = row - high
    shape = (16, row.shape[1])
    index = lax.broadcasted_iota(jnp.int32, shape, 0)
    parts = jnp.where(
        index == 0,
        jnp.broadcast_to(high, shape),
        jnp.where(index == 1, jnp.broadcast_to(low, shape), 0.0),
    )
    out = dot(parts.astype(BF16), matrix)
    return out[0:1] + out[1:2]


def as_column(row):
    return jnp.transpose(jnp.broadcast_to(row, (LANES, row.shape[1])))


def pick_row(rows, index):
    position = lax.broadcasted_iota(jnp.int32, rows.shape, 0)
    return jnp.sum(jnp.where(position == index, rows, 0.0), axis=0, keepdims=True)


def kernel(
    n, ranks, owners, tiles, cells_total,
    x_hbm, y_hbm, q_hbm, r_hbm, g_hbm, a_hbm, b_hbm, expr_hbm,
    q_hbm_out, r_hbm_out, w_hbm_out, pred_hbm_out,
    q_out, r_out, w_out, pred_out, out_sem,
    x_ref, y_ref, q_ref, r_ref, g_ref, a_ref, b_ref, expr_ref, in_sem,
    factors, part_src, part_buf, cross, vec_buf, vecs, grads_q, grads_r, grads_g,
    peaks, kq, kr, kqt, krt, t_buf, mate_kern, mate_expr, u_buf, scaled,
    prof_src, prof_buf, prof,
    part_send, part_recv, vec_send, vec_recv, cross_send, cross_recv,
    fac_send, fac_recv, rank_send, rank_recv, vr_send, vr_recv,
    peak_send, peak_recv, t_send, t_recv, mate_send, mate_recv,
    prof_send, prof_recv, gat_send, gat_recv, fwd_send, fwd_recv,
):
    me = lax.axis_index("cells")
    k = lax.axis_index("rank")
    near = k + 1 - 2 * lax.rem(k, 2)
    far = lax.rem(k + 2, 4)
    across = 3 - k
    group, half = me // 2, lax.rem(me, 2)
    groups = n // 2
    mate = me + 1 - 2 * half

    def each(first, last, body):
        if last - first <= 8:
            for i in range(first, last):
                body(i)
        else:
            def one(i, carry):
                body(i)
                return carry
            lax.fori_loop(first, last, one, 0)

    def others(index, count):
        if count > 8 or count & (count - 1):
            return lambda body, reverse=False: each(
                1, count, lambda offset: body(lax.rem(index + offset, count))
            )
        found = []
        for offset in range(count - 1, 0, -1):
            other = index
            for bit in (1, 2, 4):
                if offset & bit:
                    other = other + bit - 2 * bit * lax.rem(index // bit, 2)
            found.append(other)

        def over(body, reverse=False):
            for other in found[::-1] if reverse else found:
                body(other)

        return over

    peers = others(me, n)
    lines = others(group, groups)

    first, line_first = (n - owners) // 2, (groups - tiles) // 2
    mine, line_mine = me - first, group - line_first

    def owner(body):
        pl.when((me >= first) & (me < first + owners))(body)

    def line_owner(body):
        pl.when((group >= line_first) & (group < line_first + tiles))(body)

    def other_owners(body):
        each(0, owners, lambda o: pl.when(first + o != me)(functools.partial(body, o)))

    def other_line_owners(body):
        each(0, tiles, lambda o: pl.when(line_first + o != group)(functools.partial(body, o)))

    def to_peer(src, dst, send, recv, j):
        return pltpu.make_async_remote_copy(
            src_ref=src, dst_ref=dst, send_sem=send, recv_sem=recv,
            device_id=(j, k), device_id_type=MESH,
        )

    def to_rank(src, dst, send, recv, other):
        return pltpu.make_async_remote_copy(
            src_ref=src, dst_ref=dst, send_sem=send, recv_sem=recv,
            device_id=(me, other), device_id_type=MESH,
        )

    def all_copies(slots, send, recv):
        most = slots.at[pl.ds(0, n - 1)]
        return to_peer(most, most, send, recv, mate)

    loads = [
        pltpu.make_async_copy(src, dst, in_sem.at[i])
        for i, (src, dst) in enumerate(
            (
                (q_hbm, q_ref), (x_hbm, x_ref), (r_hbm, r_ref), (y_hbm, y_ref),
                (g_hbm, g_ref), (a_hbm, a_ref), (b_hbm, b_ref), (expr_hbm, expr_ref),
            )
        )
    ]
    for load in loads:
        load.start()
    barrier = pltpu.get_barrier_semaphore()
    peers(lambda j: pl.semaphore_signal(barrier, inc=1, device_id=(j, k), device_id_type=MESH))
    for other in (near, far, across):
        pl.semaphore_signal(barrier, inc=1, device_id=(me, other), device_id_type=MESH)

    depth = part_src.shape[2]
    loads[0].wait()
    q = q_ref[...]
    q_round = q.astype(BF16)
    factors[k, 0] = q_round
    loads[1].wait()
    x = x_ref[...]
    part_src[:, 0] = contract_rows(x, q_round).astype(BF16).reshape(owners, depth, LANES)
    loads[2].wait()
    r = r_ref[...]
    r_round = r.astype(BF16)
    factors[k, 1] = r_round
    loads[3].wait()
    y = y_ref[...]
    part_src[:, 1] = contract_rows(y, r_round).astype(BF16).reshape(owners, depth, LANES)
    for load in loads[4:]:
        load.wait()
    pl.semaphore_wait(barrier, n - 1 + 3)

    def part_copy(o):
        return to_peer(
            part_src.at[o], part_buf.at[me], part_send.at[o], part_recv.at[me], first + o
        )

    def part_arrival(j):
        return to_peer(part_src.at[0], part_buf.at[j], part_send.at[0], part_recv.at[j], j)

    def vec_copy(j, slot):
        return to_peer(vec_buf.at[me], vec_buf.at[slot], vec_send.at[0], vec_recv.at[0], j)

    other_owners(lambda o: part_copy(o).start())

    def factor_copy(slot, i, other):
        return to_rank(factors.at[slot], factors.at[slot], fac_send.at[i], fac_recv.at[i], other)

    factor_copy(k, 0, near).start()
    factor_copy(k, 1, far).start()

    norms_one = jnp.sum(jnp.square(x.astype(F32)), axis=1, keepdims=True)
    norms_two = jnp.sum(jnp.square(y.astype(F32)), axis=1, keepdims=True)
    vec_buf[me] = jnp.concatenate(
        [
            jnp.sum(norms_one * q, axis=0, keepdims=True),
            jnp.sum(q, axis=0, keepdims=True),
            jnp.sum(norms_two * r, axis=0, keepdims=True),
            jnp.sum(r, axis=0, keepdims=True),
            jnp.zeros((4, LANES), F32),
        ],
        axis=0,
    )
    peers(lambda j: vec_copy(j, me).start())

    def cross_copy(j, o):
        return to_peer(cross.at[k, o], cross.at[k, o], cross_send.at[j], cross_recv.at[o], j)

    def rank_copy(slot, i, other, j):
        return to_rank(
            cross.at[slot, j], cross.at[slot, j], rank_send.at[i, j], rank_recv.at[i, j], other
        )

    def pass_on(j):
        rank_copy(k, 1, far, j).start()
        rank_copy(k, 0, near, j).start()

    @owner
    def reduce_parts():
        part_buf[me] = part_src[mine]
        peers(lambda j: part_arrival(j).wait_recv())
        total = part_buf[0].astype(F32)
        for j in range(1, n):
            total = total + part_buf[j].astype(F32)
        cross[k, mine] = total.astype(BF16)
        peers(lambda j: cross_copy(j, mine).start())
        pass_on(mine)

    all_copies(vec_buf, vec_send.at[0], vec_recv.at[0]).wait_recv()
    vec = vec_buf[0]
    for j in range(1, n):
        vec = vec + vec_buf[j]
    slot_row = lax.broadcasted_iota(jnp.int32, (8, LANES), 0)
    vecs[k] = jnp.where(slot_row == 4, jnp.broadcast_to(g_ref[...], (8, LANES)), vec)

    def vecs_copy(slot, i, other):
        return to_rank(vecs.at[slot], vecs.at[slot], vr_send.at[i], vr_recv.at[i], other)

    for i, other in enumerate((near, far, across)):
        vecs_copy(k, i, other).start()

    def arrived(o):
        cross_copy(first + o, o).wait_recv()
        pass_on(o)

    other_owners(arrived)
    factor_copy(far, 1, far).wait_recv()
    factor_copy(far, 2, near).start()

    def expr_copy(piece):
        size = expr_ref.shape[0] // PIECES
        rows = pl.ds(pl.multiple_of(piece * size, size), size)
        return to_peer(
            expr_ref.at[rows], mate_expr.at[rows], mate_send.at[0, piece], mate_recv.at[0, piece], mate
        )

    def kern_copy(piece):
        size = mate_kern.shape[0] // PIECES
        rows = pl.ds(pl.multiple_of(piece * size, size), size)
        return to_peer(
            krt.at[1 - half, rows], mate_kern.at[rows],
            mate_send.at[1, piece], mate_recv.at[1, piece], mate,
        )

    u_copy = to_peer(u_buf.at[0], u_buf.at[1], mate_send.at[2, 0], mate_recv.at[2, 0], mate)

    def gradients(kk):
        info = vecs[kk]
        xq_vec, cq_vec, yr_vec, cr_vec, g = (info[i : i + 1] for i in range(5))
        scale = SCALE / g
        dim = x.shape[1]
        cross_xq = cross[kk, :, 0].reshape(dim, LANES)
        cross_yr = cross[kk, :, 1].reshape(dim, LANES)
        grad_q = (norms_one * cr_vec + yr_vec - 2.0 * dot(x, cross_yr)) * scale
        grad_r = (norms_two * cq_vec + xq_vec - 2.0 * dot(y, cross_xq)) * scale
        grads_q[kk] = grad_q
        grads_r[kk] = grad_r
        inner = jnp.sum(cross_xq.astype(F32) * cross_yr.astype(F32), axis=0, keepdims=True)
        curvature = SCALE * (xq_vec * cr_vec + cq_vec * yr_vec - 2.0 * inner)
        grad_g = -curvature / jnp.square(g)
        grads_g[kk] = jnp.broadcast_to(grad_g, (8, LANES))
        return jnp.maximum(
            jnp.max(jnp.maximum(jnp.abs(grad_q), jnp.abs(grad_r)), axis=0, keepdims=True),
            jnp.abs(grad_g),
        )

    peak = gradients(k)
    vecs_copy(near, 0, near).wait_recv()
    each(0, owners, lambda j: rank_copy(near, 0, near, j).wait_recv())
    peak = jnp.maximum(peak, gradients(near))

    def across_x(j):
        rank_copy(far, 1, far, j).wait_recv()
        rank_copy(far, 2, near, j).start()

    each(0, owners, across_x)
    vecs_copy(far, 1, far).wait_recv()
    peak = jnp.maximum(peak, gradients(far))
    vecs_copy(across, 2, across).wait_recv()
    each(0, owners, lambda j: rank_copy(across, 2, near, j).wait_recv())
    peak = jnp.maximum(peak, gradients(across))
    peaks[me] = jnp.broadcast_to(peak, (8, LANES))

    def peak_copy(j, slot):
        return to_peer(peaks.at[me], peaks.at[slot], peak_send.at[0], peak_recv.at[0], j)

    peers(lambda j: peak_copy(j, me).start())
    factor_copy(near, 0, near).wait_recv()
    factor_copy(across, 2, near).wait_recv()
    log_a, log_b = jnp.log(a_ref[...]), jnp.log(b_ref[...])
    all_copies(peaks, peak_send.at[0], peak_recv.at[0]).wait_recv()
    top = peaks[0]
    for j in range(1, n):
        top = jnp.maximum(top, peaks[j])
    eta = GAMMA / (jnp.max(top, axis=1, keepdims=True)[0:1] + 1e-6)

    log_g = []
    for kk in range(ranks):
        columns = slice(kk * LANES, (kk + 1) * LANES)
        kern_q = factors[kk, 0].astype(F32) * jnp.exp(-eta * grads_q[kk])
        kern_r = factors[kk, 1].astype(F32) * jnp.exp(-eta * grads_r[kk])
        kern_q, kern_r = kern_q.astype(BF16), kern_r.astype(BF16)
        kq[:, columns] = kern_q
        kr[:, columns] = kern_r
        kqt[columns, :] = jnp.transpose(kern_q)
        rows = slice(kk % 2 * LANES, (kk % 2 + 1) * LANES)
        krt[kk // 2, rows, :] = jnp.transpose(kern_r)
        log_g.append(jnp.log(vecs[kk][4:5]) - eta * grads_g[kk][0:1])
    log_kern_g = jnp.concatenate(log_g + log_g, axis=0)

    def t_copy(parity, j, slot):
        return to_peer(
            t_buf.at[parity, me], t_buf.at[parity, slot],
            t_send.at[parity], t_recv.at[parity], j,
        )

    def t_all(parity):
        return all_copies(t_buf.at[parity], t_send.at[parity], t_recv.at[parity])

    def whole_krt():
        return krt[...].reshape(ranks * LANES, krt.shape[2])

    def marginals(v):
        s_r = row_product(wide(v, ranks, ranks), whole_krt())
        u_r = jnp.exp(POWER * (log_b - jnp.log(s_r)))
        s_q = row_product(wide(v, 0, ranks), kqt[...])
        u_q = jnp.exp(POWER * (log_a - jnp.log(s_q)))
        return u_q, u_r

    def send_t(parity, u_q, u_r):
        t_buf[parity, me] = tall(row_product(u_q, kq[...]), row_product(u_r, kr[...]))
        peers(lambda j: t_copy(parity, j, me).start())

    def new_weights(parity, v):
        t_all(parity).wait_recv()
        t = t_buf[parity, 0]
        for j in range(1, n):
            t = t + t_buf[parity, j]
        t_all(parity).wait_send()
        logs = jnp.log(v * t)
        other = jnp.concatenate([logs[ranks:], logs[:ranks]], axis=0)
        weights = jnp.exp((log_kern_g + logs + other) / 3.0)
        return weights / t, weights, t

    def one_pass(step, v):
        parity = lax.rem(step, 2)
        send_t(parity, *marginals(v))

        @pl.when(step < PIECES)
        def send_piece():
            expr_copy(step).start()
            kern_copy(step).start()

        return new_weights(parity, v)[0]

    v = lax.fori_loop(0, PASSES - 1, one_pass, jnp.ones((2 * ranks, LANES), F32))
    u_q, u_r = marginals(v)
    u_buf[0] = u_r
    u_copy.start()
    send_t((PASSES - 1) % 2, u_q, u_r)

    def prof_copy(o, piece):
        return to_peer(
            prof_src.at[o, piece], prof_buf.at[group, piece],
            prof_send.at[o, piece], prof_recv.at[group, piece], 2 * (line_first + o) + half,
        )

    def prof_arrival(line, piece):
        return to_peer(
            prof_src.at[0, piece], prof_buf.at[line, piece],
            prof_send.at[0, piece], prof_recv.at[line, piece], 2 * line + half,
        )

    left = (krt[half].astype(F32) * u_r).astype(BF16)
    total = dot(left, expr_ref[...])
    for piece in range(PIECES):
        expr_copy(piece).wait_recv()
        kern_copy(piece).wait_recv()
    u_copy.wait_recv()
    left = (mate_kern[...].astype(F32) * u_buf[1]).astype(BF16)
    total = total + dot(left, mate_expr[...])
    prof_src[...] = total.astype(BF16).reshape(prof_src.shape)
    for piece in range(HALVES):
        other_line_owners(lambda o: prof_copy(o, piece).start())

    @line_owner
    def own_prof():
        prof_buf[group] = prof_src[line_mine]

    v, weights, t = new_weights((PASSES - 1) % 2, v)

    other_owners(lambda o: part_copy(o).wait_send())

    @owner
    def cross_sends():
        peers(lambda j: cross_copy(j, mine).wait_send())

    all_copies(vec_buf, vec_send.at[0], vec_recv.at[0]).wait_send()
    all_copies(peaks, peak_send.at[0], peak_recv.at[0]).wait_send()
    for i, (slot, other) in enumerate(((k, near), (k, far), (far, near))):
        factor_copy(slot, i, other).wait_send()
        each(0, owners, lambda j: rank_copy(slot, i, other, j).wait_send())
    for i, other in enumerate((near, far, across)):
        vecs_copy(k, i, other).wait_send()
    u_copy.wait_send()
    for piece in range(PIECES):
        expr_copy(piece).wait_send()
        kern_copy(piece).wait_send()
    w_out[...] = pick_row(weights, k) / cells_total
    own_q = q_ref[...] * jnp.exp(-eta * grads_q[k])
    own_r = r_ref[...] * jnp.exp(-eta * grads_r[k])
    q_out[...] = as_column(u_q) * own_q * pick_row(v, k)
    r_out[...] = as_column(u_r) * own_r * pick_row(v, k + ranks)
    def block_rows(i):
        size = pred_out.shape[0] // BLOCKS
        return slice(i * size, (i + 1) * size)

    stores = [
        pltpu.make_async_copy(src, dst, out_sem.at[i])
        for i, (src, dst) in enumerate(
            (
                (q_out, q_hbm_out), (r_out, r_hbm_out),
                (w_out, w_hbm_out),
            )
            + tuple(
                (pred_out.at[block_rows(i)], pred_hbm_out.at[block_rows(i)])
                for i in range(BLOCKS)
            )
        )
    ]
    for store in stores[:3]:
        store.start()
    inverse = as_column(1.0 / row_product(wide(v, 0, ranks), kqt[...]))
    ratio = wide(v[ranks:] / t[:ranks], 0, ranks)
    width = scaled.shape[2]
    for i in range(2):
        columns = slice(i * width, (i + 1) * width)
        scaled[i] = (kq[:, columns].astype(F32) * ratio[:, columns]).astype(BF16)

    def gather_copy(line, o, piece):
        return to_peer(
            prof.at[half, o, piece], prof.at[half, o, piece],
            gat_send.at[line, piece], gat_recv.at[o, piece], 2 * line + half,
        )

    def forward_copy(side, o, piece):
        return to_peer(
            prof.at[side, o, piece], prof.at[side, o, piece],
            fwd_send.at[o, piece], fwd_recv.at[o, piece], mate,
        )

    @line_owner
    def reduce_prof():
        for piece in range(HALVES):
            lines(lambda line: prof_arrival(line, piece).wait_recv())
            total = prof_buf[0, piece].astype(F32)
            for line in range(1, groups):
                total = total + prof_buf[line, piece].astype(F32)
            prof[half, line_mine, piece] = total.astype(BF16)
            lines(lambda line: gather_copy(line, line_mine, piece).start())
            forward_copy(half, line_mine, piece).start()

    def gathered(o, piece):
        gather_copy(line_first + o, o, piece).wait_recv()
        forward_copy(half, o, piece).start()

    for piece in range(HALVES):
        other_line_owners(lambda o: gathered(o, piece))
    flat = (scaled.shape[2], prof.shape[4])
    for piece in range(HALVES):
        each(0, tiles, lambda o: forward_copy(1 - half, o, piece).wait_recv())
    for i in range(BLOCKS):
        rows = block_rows(i)
        mixed = dot(scaled[half, rows], prof[half].reshape(flat))
        mixed = mixed + dot(scaled[1 - half, rows], prof[1 - half].reshape(flat))
        across_genes = jnp.concatenate([inverse[rows]] * (mixed.shape[1] // LANES), axis=1)
        pred_out[rows] = (mixed * across_genes).astype(BF16)
        stores[3 + i].start()

    for piece in range(HALVES):
        other_line_owners(lambda o: prof_copy(o, piece).wait_send())
        each(0, tiles, lambda o: forward_copy(half, o, piece).wait_send())

    @line_owner
    def gather_sends():
        for piece in range(HALVES):
            lines(lambda line: gather_copy(line, line_mine, piece).wait_send())

    for store in stores:
        store.wait()


def write_out(count, *refs):
    sources, results, held = (refs[i * count : (i + 1) * count] for i in range(3))
    load_sem, store_sem = refs[3 * count :]
    loads, stores = [], []
    for source, result, hold in zip(sources, results, held):
        pieces = BLOCKS if source.shape[0] > BLOCKS else 1
        size = source.shape[0] // pieces
        for i in range(pieces):
            rows = pl.ds(i * size, size)
            sem = len(loads)
            loads.append(
                pltpu.make_async_copy(source.at[rows], hold.at[rows], load_sem.at[sem])
            )
            stores.append(
                pltpu.make_async_copy(hold.at[rows], result.at[rows], store_sem.at[sem])
            )
    for load in loads:
        load.start()
    for load, store in zip(loads, stores):
        load.wait()
        store.start()
    for store in stores:
        store.wait()


def shards(n, ranks, x_emb, y_emb, q_factor, r_factor, g_weights, a_mass, b_mass, expr):
    rows, dim = x_emb.shape
    genes = expr.shape[1]
    rank_all = ranks * LANES
    owners = min(n // 2, dim // 16)
    groups = n // 2
    tiles = min(groups // 2, rank_all // 2 // (16 * HALVES))
    hbm = pl.BlockSpec(memory_space=pltpu.HBM)
    dma = pltpu.SemaphoreType.DMA
    pair = [dma((n,)), dma((n,))]
    single = [dma((1,)), dma((1,))]
    three = [dma((3,)), dma((3,))]
    lined = [dma((groups, HALVES)), dma((groups, HALVES))]
    block = (HALVES, rank_all // 2 // tiles // HALVES, genes)
    shapes = (
        jax.ShapeDtypeStruct(q_factor.shape, F32),
        jax.ShapeDtypeStruct(r_factor.shape, F32),
        jax.ShapeDtypeStruct((1, LANES), F32),
        jax.ShapeDtypeStruct((rows, genes), BF16),
    )
    results = pl.pallas_call(
        functools.partial(kernel, n, ranks, owners, tiles, float(rows * n)),
        out_shape=shapes,
        in_specs=[hbm] * 8,
        out_specs=(hbm,) * 4,
        scratch_shapes=[
            pltpu.VMEM(q_factor.shape, F32),
            pltpu.VMEM(r_factor.shape, F32),
            pltpu.VMEM((1, LANES), F32),
            pltpu.VMEM((rows, genes), BF16),
            dma((3 + BLOCKS,)),
            pltpu.VMEM(x_emb.shape, BF16),
            pltpu.VMEM(y_emb.shape, BF16),
            pltpu.VMEM(q_factor.shape, F32),
            pltpu.VMEM(r_factor.shape, F32),
            pltpu.VMEM((1, LANES), F32),
            pltpu.VMEM((1, rows), F32),
            pltpu.VMEM((1, rows), F32),
            pltpu.VMEM(expr.shape, BF16),
            dma((8,)),
            pltpu.VMEM((ranks, 2, rows, LANES), BF16),
            pltpu.VMEM((owners, 2, dim // owners, LANES), BF16),
            pltpu.VMEM((n, 2, dim // owners, LANES), BF16),
            pltpu.VMEM((ranks, owners, 2, dim // owners, LANES), BF16),
            pltpu.VMEM((n, 8, LANES), F32),
            pltpu.VMEM((ranks, 8, LANES), F32),
            pltpu.VMEM((ranks, rows, LANES), F32),
            pltpu.VMEM((ranks, rows, LANES), F32),
            pltpu.VMEM((ranks, 8, LANES), F32),
            pltpu.VMEM((n, 8, LANES), F32),
            pltpu.VMEM((rows, rank_all), BF16),
            pltpu.VMEM((rows, rank_all), BF16),
            pltpu.VMEM((rank_all, rows), BF16),
            pltpu.VMEM((2, rank_all // 2, rows), BF16),
            pltpu.VMEM((2, n, 8, LANES), F32),
            pltpu.VMEM((rank_all // 2, rows), BF16),
            pltpu.VMEM(expr.shape, BF16),
            pltpu.VMEM((2, 1, rows), F32),
            pltpu.VMEM((2, rows, rank_all // 2), BF16),
            pltpu.VMEM((tiles,) + block, BF16),
            pltpu.VMEM((groups,) + block, BF16),
            pltpu.VMEM((2, tiles) + block, BF16),
        ]
        + pair + single + pair + three
        + [dma((3, owners)), dma((3, owners))]
        + three + single
        + [dma((2,)), dma((2,))]
        + [dma((3, PIECES)), dma((3, PIECES))]
        + lined + lined + lined,
        compiler_params=pltpu.CompilerParams(
            collective_id=0, has_side_effects=True, vmem_limit_bytes=VMEM_LIMIT
        ),
        cost_estimate=pl.CostEstimate(
            flops=2 * rows * (2 * dim * LANES + 2 * dim * rank_all + 2 * rank_all * genes),
            bytes_accessed=4 * 1024 * 1024,
            transcendentals=2 * rows * rank_all,
        ),
        name="transport_step",
    )(
        x_emb, y_emb, q_factor, r_factor, g_weights.reshape(1, LANES),
        a_mass.reshape(1, rows), b_mass.reshape(1, rows), expr,
    )
    q_new, r_new, rank_share, predicted = pl.pallas_call(
        functools.partial(write_out, len(shapes)),
        out_shape=shapes,
        in_specs=[hbm] * 4,
        out_specs=(hbm,) * 4,
        scratch_shapes=[pltpu.VMEM(shape.shape, shape.dtype) for shape in shapes]
        + [dma((len(shapes) * BLOCKS,)), dma((len(shapes) * BLOCKS,))],
        compiler_params=pltpu.CompilerParams(vmem_limit_bytes=VMEM_LIMIT),
        name="write_out",
    )(*results)
    return q_new, r_new, rank_share.reshape(LANES), predicted


def solution(mesh):
    n, ranks = mesh.shape["cells"], mesh.shape["rank"]
    assert ranks == 4
    return jax.shard_map(
        functools.partial(shards, n, ranks),
        mesh=mesh,
        in_specs=(
            P("cells", None),
            P("cells", None),
            P("cells", "rank"),
            P("cells", "rank"),
            P("rank"),
            P("cells"),
            P("cells"),
            P("cells", "rank"),
        ),
        out_specs=(P("cells", "rank"), P("cells", "rank"), P("rank"), P("cells", "rank")),
        check_vma=False,
    )
```

```python
import functools

import jax
import jax.numpy as jnp
from jax import lax
from jax.experimental import pallas as pl
from jax.experimental.pallas import tpu as pltpu
from jax.sharding import PartitionSpec as P

PASSES = 10
PIECES = 8
BLOCKS = 4
HALVES = 2
SCALE = 0.0625
GAMMA = 10.0
POWER = 0.8
LANES = 128
VMEM_LIMIT = 56 * 1024 * 1024
MESH = pl.DeviceIdType.MESH
F32 = jnp.float32
BF16 = jnp.bfloat16


def dot(left, right):
    return jnp.dot(left, right, preferred_element_type=F32)


def contract_rows(left, right):
    return lax.dot_general(
        left, right, (((0,), (0,)), ((), ())), preferred_element_type=F32
    )


def wide(rows, first, count):
    return jnp.concatenate([rows[first + i : first + i + 1] for i in range(count)], axis=1)


def tall(*rows):
    return jnp.concatenate(
        [row[:, i * LANES : (i + 1) * LANES] for row in rows for i in range(row.shape[1] // LANES)],
        axis=0,
    )


def row_product(row, matrix):
    high = row.astype(BF16).astype(F32)
    low = row - high
    shape = (16, row.shape[1])
    index = lax.broadcasted_iota(jnp.int32, shape, 0)
    parts = jnp.where(
        index == 0,
        jnp.broadcast_to(high, shape),
        jnp.where(index == 1, jnp.broadcast_to(low, shape), 0.0),
    )
    out = dot(parts.astype(BF16), matrix)
    return out[0:1] + out[1:2]


def as_column(row):
    return jnp.transpose(jnp.broadcast_to(row, (LANES, row.shape[1])))


def pick_row(rows, index):
    position = lax.broadcasted_iota(jnp.int32, rows.shape, 0)
    return jnp.sum(jnp.where(position == index, rows, 0.0), axis=0, keepdims=True)


def kernel(
    n, ranks, owners, tiles, cells_total,
    x_hbm, y_hbm, q_hbm, r_hbm, g_hbm, a_hbm, b_hbm, expr_hbm,
    q_hbm_out, r_hbm_out, w_hbm_out, pred_hbm_out,
    q_out, r_out, w_out, pred_out, out_sem,
    x_ref, y_ref, q_ref, r_ref, g_ref, a_ref, b_ref, expr_ref, in_sem,
    factors, part_src, part_buf, cross, vec_buf, vecs, grads_q, grads_r, grads_g,
    factors_t, grads_t, peaks, kq, kr, kqt, krt, t_buf, mate_kern, mate_expr, u_buf, scaled,
    prof_src, prof_buf, prof,
    part_send, part_recv, vec_send, vec_recv, cross_send, cross_recv,
    fac_send, fac_recv, rank_send, rank_recv, vr_send, vr_recv,
    peak_send, peak_recv, t_send, t_recv, mate_send, mate_recv,
    prof_send, prof_recv, gat_send, gat_recv, fwd_send, fwd_recv,
):
    me = lax.axis_index("cells")
    k = lax.axis_index("rank")
    near = k + 1 - 2 * lax.rem(k, 2)
    far = lax.rem(k + 2, 4)
    across = 3 - k
    group, half = me // 2, lax.rem(me, 2)
    groups = n // 2
    mate = me + 1 - 2 * half

    def each(first, last, body):
        if last - first <= 8:
            for i in range(first, last):
                body(i)
        else:
            def one(i, carry):
                body(i)
                return carry
            lax.fori_loop(first, last, one, 0)

    def others(index, count):
        if count > 8 or count & (count - 1):
            return lambda body, reverse=False: each(
                1, count, lambda offset: body(lax.rem(index + offset, count))
            )
        found = []
        for offset in range(count - 1, 0, -1):
            other = index
            for bit in (1, 2, 4):
                if offset & bit:
                    other = other + bit - 2 * bit * lax.rem(index // bit, 2)
            found.append(other)

        def over(body, reverse=False):
            for other in found[::-1] if reverse else found:
                body(other)

        return over

    peers = others(me, n)
    lines = others(group, groups)

    first, line_first = (n - owners) // 2, (groups - tiles) // 2
    mine, line_mine = me - first, group - line_first

    def owner(body):
        pl.when((me >= first) & (me < first + owners))(body)

    def line_owner(body):
        pl.when((group >= line_first) & (group < line_first + tiles))(body)

    def other_owners(body):
        each(0, owners, lambda o: pl.when(first + o != me)(functools.partial(body, o)))

    def other_line_owners(body):
        each(0, tiles, lambda o: pl.when(line_first + o != group)(functools.partial(body, o)))

    def to_peer(src, dst, send, recv, j):
        return pltpu.make_async_remote_copy(
            src_ref=src, dst_ref=dst, send_sem=send, recv_sem=recv,
            device_id=(j, k), device_id_type=MESH,
        )

    def to_rank(src, dst, send, recv, other):
        return pltpu.make_async_remote_copy(
            src_ref=src, dst_ref=dst, send_sem=send, recv_sem=recv,
            device_id=(me, other), device_id_type=MESH,
        )

    def all_copies(slots, send, recv):
        most = slots.at[pl.ds(0, n - 1)]
        return to_peer(most, most, send, recv, mate)

    barrier = pltpu.get_barrier_semaphore()
    peers(lambda j: pl.semaphore_signal(barrier, inc=1, device_id=(j, k), device_id_type=MESH))
    for other in (near, far, across):
        pl.semaphore_signal(barrier, inc=1, device_id=(me, other), device_id_type=MESH)

    loads = [
        pltpu.make_async_copy(src, dst, in_sem.at[i])
        for i, (src, dst) in enumerate(
            (
                (q_hbm, q_ref), (x_hbm, x_ref), (r_hbm, r_ref), (y_hbm, y_ref),
                (g_hbm, g_ref), (a_hbm, a_ref), (b_hbm, b_ref), (expr_hbm, expr_ref),
            )
        )
    ]
    for load in loads:
        load.start()

    depth = part_src.shape[2]
    loads[0].wait()
    q = q_ref[...]
    q_round = q.astype(BF16)
    factors[k, 0] = q_round
    loads[1].wait()
    x = x_ref[...]
    part_src[:, 0] = contract_rows(x, q_round).astype(BF16).reshape(owners, depth, LANES)
    loads[2].wait()
    r = r_ref[...]
    r_round = r.astype(BF16)
    factors[k, 1] = r_round
    loads[3].wait()
    y = y_ref[...]
    part_src[:, 1] = contract_rows(y, r_round).astype(BF16).reshape(owners, depth, LANES)
    for load in loads[4:]:
        load.wait()
    pl.semaphore_wait(barrier, n - 1 + 3)

    def part_copy(o):
        return to_peer(
            part_src.at[o], part_buf.at[me], part_send.at[o], part_recv.at[me], first + o
        )

    def part_arrival(j):
        return to_peer(part_src.at[0], part_buf.at[j], part_send.at[0], part_recv.at[j], j)

    def vec_copy(j, slot):
        return to_peer(vec_buf.at[me], vec_buf.at[slot], vec_send.at[0], vec_recv.at[0], j)

    other_owners(lambda o: part_copy(o).start())

    def factor_copy(slot, i, other):
        return to_rank(factors.at[slot], factors.at[slot], fac_send.at[i], fac_recv.at[i], other)

    factor_copy(k, 0, near).start()
    factor_copy(k, 1, far).start()

    norms_one = jnp.sum(jnp.square(x.astype(F32)), axis=1, keepdims=True)
    norms_two = jnp.sum(jnp.square(y.astype(F32)), axis=1, keepdims=True)
    vec_buf[me] = jnp.concatenate(
        [
            jnp.sum(norms_one * q, axis=0, keepdims=True),
            jnp.sum(q, axis=0, keepdims=True),
            jnp.sum(norms_two * r, axis=0, keepdims=True),
            jnp.sum(r, axis=0, keepdims=True),
            jnp.zeros((4, LANES), F32),
        ],
        axis=0,
    )
    peers(lambda j: vec_copy(j, me).start())

    def cross_copy(j, o):
        return to_peer(cross.at[k, o], cross.at[k, o], cross_send.at[j], cross_recv.at[o], j)

    def rank_copy(slot, i, other, j):
        return to_rank(
            cross.at[slot, j], cross.at[slot, j], rank_send.at[i, j], rank_recv.at[i, j], other
        )

    def pass_on(j):
        rank_copy(k, 1, far, j).start()
        rank_copy(k, 0, near, j).start()

    @owner
    def reduce_parts():
        part_buf[me] = part_src[mine]
        peers(lambda j: part_arrival(j).wait_recv())
        total = part_buf[0].astype(F32)
        for j in range(1, n):
            total = total + part_buf[j].astype(F32)
        cross[k, mine] = total.astype(BF16)
        peers(lambda j: cross_copy(j, mine).start())
        pass_on(mine)

    all_copies(vec_buf, vec_send.at[0], vec_recv.at[0]).wait_recv()
    vec = vec_buf[0]
    for j in range(1, n):
        vec = vec + vec_buf[j]
    slot_row = lax.broadcasted_iota(jnp.int32, (8, LANES), 0)
    vecs[k] = jnp.where(slot_row == 4, jnp.broadcast_to(g_ref[...], (8, LANES)), vec)

    def vecs_copy(slot, i, other):
        return to_rank(vecs.at[slot], vecs.at[slot], vr_send.at[i], vr_recv.at[i], other)

    for i, other in enumerate((near, far, across)):
        vecs_copy(k, i, other).start()

    def arrived(o):
        cross_copy(first + o, o).wait_recv()
        pass_on(o)

    other_owners(arrived)
    factor_copy(far, 1, far).wait_recv()
    factor_copy(far, 2, near).start()

    def expr_copy(piece):
        size = expr_ref.shape[0] // PIECES
        rows = pl.ds(pl.multiple_of(piece * size, size), size)
        return to_peer(
            expr_ref.at[rows], mate_expr.at[rows], mate_send.at[0, piece], mate_recv.at[0, piece], mate
        )

    def kern_copy(piece):
        size = mate_kern.shape[0] // PIECES
        rows = pl.ds(pl.multiple_of(piece * size, size), size)
        return to_peer(
            krt.at[1 - half, rows], mate_kern.at[rows],
            mate_send.at[1, piece], mate_recv.at[1, piece], mate,
        )

    u_copy = to_peer(u_buf.at[0], u_buf.at[1], mate_send.at[2, 0], mate_recv.at[2, 0], mate)

    def gradients(kk):
        info = vecs[kk]
        xq_vec, cq_vec, yr_vec, cr_vec, g = (info[i : i + 1] for i in range(5))
        scale = SCALE / g
        dim = x.shape[1]
        cross_xq = cross[kk, :, 0].reshape(dim, LANES)
        cross_yr = cross[kk, :, 1].reshape(dim, LANES)
        grad_q = (norms_one * cr_vec + yr_vec - 2.0 * dot(x, cross_yr)) * scale
        grad_r = (norms_two * cq_vec + xq_vec - 2.0 * dot(y, cross_xq)) * scale
        grads_q[kk] = grad_q
        grads_r[kk] = grad_r
        inner = jnp.sum(cross_xq.astype(F32) * cross_yr.astype(F32), axis=0, keepdims=True)
        curvature = SCALE * (xq_vec * cr_vec + cq_vec * yr_vec - 2.0 * inner)
        grad_g = -curvature / jnp.square(g)
        grads_g[kk] = jnp.broadcast_to(grad_g, (8, LANES))
        return jnp.maximum(
            jnp.max(jnp.maximum(jnp.abs(grad_q), jnp.abs(grad_r)), axis=0, keepdims=True),
            jnp.abs(grad_g),
        )

    peak = gradients(k)
    vecs_copy(near, 0, near).wait_recv()
    each(0, owners, lambda j: rank_copy(near, 0, near, j).wait_recv())
    peak = jnp.maximum(peak, gradients(near))

    def across_x(j):
        rank_copy(far, 1, far, j).wait_recv()
        rank_copy(far, 2, near, j).start()

    each(0, owners, across_x)
    vecs_copy(far, 1, far).wait_recv()
    peak = jnp.maximum(peak, gradients(far))
    vecs_copy(across, 2, across).wait_recv()
    each(0, owners, lambda j: rank_copy(across, 2, near, j).wait_recv())
    peak = jnp.maximum(peak, gradients(across))
    peaks[me] = jnp.broadcast_to(peak, (8, LANES))

    def peak_copy(j, slot):
        return to_peer(peaks.at[me], peaks.at[slot], peak_send.at[0], peak_recv.at[0], j)

    peers(lambda j: peak_copy(j, me).start())
    factor_copy(near, 0, near).wait_recv()
    factor_copy(across, 2, near).wait_recv()
    log_a, log_b = jnp.log(a_ref[...]), jnp.log(b_ref[...])
    for kk in range(ranks):
        grads_t[kk, 0] = jnp.transpose(grads_q[kk])
        grads_t[kk, 1] = jnp.transpose(grads_r[kk])
        factors_t[kk, 0] = jnp.transpose(factors[kk, 0])
        factors_t[kk, 1] = jnp.transpose(factors[kk, 1])
    all_copies(peaks, peak_send.at[0], peak_recv.at[0]).wait_recv()
    top = peaks[0]
    for j in range(1, n):
        top = jnp.maximum(top, peaks[j])
    eta = GAMMA / (jnp.max(top, axis=1, keepdims=True)[0:1] + 1e-6)

    log_g = []
    for kk in range(ranks):
        columns = slice(kk * LANES, (kk + 1) * LANES)
        kern_q = factors[kk, 0].astype(F32) * jnp.exp(-eta * grads_q[kk])
        kern_r = factors[kk, 1].astype(F32) * jnp.exp(-eta * grads_r[kk])
        kq[:, columns] = kern_q.astype(BF16)
        kr[:, columns] = kern_r.astype(BF16)
        kern_qt, kern_rt = (
            factors_t[kk, i].astype(F32) * jnp.exp(-eta * grads_t[kk, i]) for i in range(2)
        )
        kqt[columns, :] = kern_qt.astype(BF16)
        rows = slice(kk % 2 * LANES, (kk % 2 + 1) * LANES)
        krt[kk // 2, rows, :] = kern_rt.astype(BF16)
        log_g.append(jnp.log(vecs[kk][4:5]) - eta * grads_g[kk][0:1])
    log_kern_g = jnp.concatenate(log_g + log_g, axis=0)

    def t_copy(parity, j, slot):
        return to_peer(
            t_buf.at[parity, me], t_buf.at[parity, slot],
            t_send.at[parity], t_recv.at[parity], j,
        )

    def t_all(parity):
        return all_copies(t_buf.at[parity], t_send.at[parity], t_recv.at[parity])

    def marginals(v):
        s_r = row_product(wide(v, ranks, ranks // 2), krt[0])
        s_r = s_r + row_product(wide(v, ranks + ranks // 2, ranks // 2), krt[1])
        u_r = jnp.exp(POWER * (log_b - jnp.log(s_r)))
        s_q = row_product(wide(v, 0, ranks), kqt[...])
        u_q = jnp.exp(POWER * (log_a - jnp.log(s_q)))
        return u_q, u_r

    def send_t(parity, u_q, u_r):
        t_buf[parity, me] = tall(row_product(u_q, kq[...]), row_product(u_r, kr[...]))
        peers(lambda j: t_copy(parity, j, me).start())

    def new_weights(parity, v):
        t_all(parity).wait_recv()
        t = t_buf[parity, 0]
        for j in range(1, n):
            t = t + t_buf[parity, j]
        t_all(parity).wait_send()
        logs = jnp.log(v * t)
        other = jnp.concatenate([logs[ranks:], logs[:ranks]], axis=0)
        weights = jnp.exp((log_kern_g + logs + other) / 3.0)
        return weights / t, weights, t

    def one_pass(step, v):
        parity = lax.rem(step, 2)
        send_t(parity, *marginals(v))

        @pl.when(step < PIECES)
        def send_piece():
            expr_copy(step).start()
            kern_copy(step).start()

        return new_weights(parity, v)[0]

    v = lax.fori_loop(0, PASSES - 1, one_pass, jnp.ones((2 * ranks, LANES), F32))
    u_q, u_r = marginals(v)
    u_buf[0] = u_r
    u_copy.start()
    send_t((PASSES - 1) % 2, u_q, u_r)

    def prof_copy(o, piece):
        return to_peer(
            prof_src.at[o, piece], prof_buf.at[group, piece],
            prof_send.at[o, piece], prof_recv.at[group, piece], 2 * (line_first + o) + half,
        )

    def prof_arrival(line, piece):
        return to_peer(
            prof_src.at[0, piece], prof_buf.at[line, piece],
            prof_send.at[0, piece], prof_recv.at[line, piece], 2 * line + half,
        )

    left = (krt[half].astype(F32) * u_r).astype(BF16)
    total = dot(left, expr_ref[...])
    for piece in range(PIECES):
        expr_copy(piece).wait_recv()
        kern_copy(piece).wait_recv()
    u_copy.wait_recv()
    left = (mate_kern[...].astype(F32) * u_buf[1]).astype(BF16)
    total = total + dot(left, mate_expr[...])
    prof_src[...] = total.astype(BF16).reshape(prof_src.shape)
    for piece in range(HALVES):
        other_line_owners(lambda o: prof_copy(o, piece).start())

    @line_owner
    def own_prof():
        prof_buf[group] = prof_src[line_mine]

    v, weights, t = new_weights((PASSES - 1) % 2, v)

    other_owners(lambda o: part_copy(o).wait_send())

    @owner
    def cross_sends():
        peers(lambda j: cross_copy(j, mine).wait_send())

    all_copies(vec_buf, vec_send.at[0], vec_recv.at[0]).wait_send()
    all_copies(peaks, peak_send.at[0], peak_recv.at[0]).wait_send()
    for i, (slot, other) in enumerate(((k, near), (k, far), (far, near))):
        factor_copy(slot, i, other).wait_send()
        each(0, owners, lambda j: rank_copy(slot, i, other, j).wait_send())
    for i, other in enumerate((near, far, across)):
        vecs_copy(k, i, other).wait_send()
    u_copy.wait_send()
    for piece in range(PIECES):
        expr_copy(piece).wait_send()
        kern_copy(piece).wait_send()
    w_out[...] = pick_row(weights, k) / cells_total
    own_q = q_ref[...] * jnp.exp(-eta * grads_q[k])
    own_r = r_ref[...] * jnp.exp(-eta * grads_r[k])
    q_out[...] = as_column(u_q) * own_q * pick_row(v, k)
    r_out[...] = as_column(u_r) * own_r * pick_row(v, k + ranks)
    def block_rows(i):
        size = pred_out.shape[0] // BLOCKS
        return slice(i * size, (i + 1) * size)

    stores = [
        pltpu.make_async_copy(src, dst, out_sem.at[i])
        for i, (src, dst) in enumerate(
            (
                (q_out, q_hbm_out), (r_out, r_hbm_out),
                (w_out, w_hbm_out),
            )
            + tuple(
                (pred_out.at[block_rows(i)], pred_hbm_out.at[block_rows(i)])
                for i in range(BLOCKS)
            )
        )
    ]
    for store in stores[:3]:
        store.start()
    inverse = as_column(1.0 / row_product(wide(v, 0, ranks), kqt[...]))
    ratio = wide(v[ranks:] / t[:ranks], 0, ranks)
    width = scaled.shape[2]
    for i in range(2):
        columns = slice(i * width, (i + 1) * width)
        scaled[i] = (kq[:, columns].astype(F32) * ratio[:, columns]).astype(BF16)

    def gather_copy(line, o, piece):
        return to_peer(
            prof.at[half, o, piece], prof.at[half, o, piece],
            gat_send.at[line, piece], gat_recv.at[o, piece], 2 * line + half,
        )

    def forward_copy(side, o, piece):
        return to_peer(
            prof.at[side, o, piece], prof.at[side, o, piece],
            fwd_send.at[o, piece], fwd_recv.at[o, piece], mate,
        )

    @line_owner
    def reduce_prof():
        for piece in range(HALVES):
            lines(lambda line: prof_arrival(line, piece).wait_recv())
            total = prof_buf[0, piece].astype(F32)
            for line in range(1, groups):
                total = total + prof_buf[line, piece].astype(F32)
            prof[half, line_mine, piece] = total.astype(BF16)
            lines(lambda line: gather_copy(line, line_mine, piece).start())
            forward_copy(half, line_mine, piece).start()

    def gathered(o, piece):
        gather_copy(line_first + o, o, piece).wait_recv()
        forward_copy(half, o, piece).start()

    for piece in range(HALVES):
        other_line_owners(lambda o: gathered(o, piece))
    flat = (scaled.shape[2], prof.shape[4])
    for piece in range(HALVES):
        each(0, tiles, lambda o: forward_copy(1 - half, o, piece).wait_recv())
    for i in range(BLOCKS):
        rows = block_rows(i)
        mixed = dot(scaled[half, rows], prof[half].reshape(flat))
        mixed = mixed + dot(scaled[1 - half, rows], prof[1 - half].reshape(flat))
        across_genes = jnp.concatenate([inverse[rows]] * (mixed.shape[1] // LANES), axis=1)
        pred_out[rows] = (mixed * across_genes).astype(BF16)
        stores[3 + i].start()

    for piece in range(HALVES):
        other_line_owners(lambda o: prof_copy(o, piece).wait_send())
        each(0, tiles, lambda o: forward_copy(half, o, piece).wait_send())

    @line_owner
    def gather_sends():
        for piece in range(HALVES):
            lines(lambda line: gather_copy(line, line_mine, piece).wait_send())

    for store in stores:
        store.wait()


def write_out(count, *refs):
    sources, results, held = (refs[i * count : (i + 1) * count] for i in range(3))
    load_sem, store_sem = refs[3 * count :]
    loads, stores = [], []
    for source, result, hold in zip(sources, results, held):
        pieces = BLOCKS if source.shape[0] > BLOCKS else 1
        size = source.shape[0] // pieces
        for i in range(pieces):
            rows = pl.ds(i * size, size)
            sem = len(loads)
            loads.append(
                pltpu.make_async_copy(source.at[rows], hold.at[rows], load_sem.at[sem])
            )
            stores.append(
                pltpu.make_async_copy(hold.at[rows], result.at[rows], store_sem.at[sem])
            )
    for load in loads:
        load.start()
    for load, store in zip(loads, stores):
        load.wait()
        store.start()
    for store in stores:
        store.wait()


def shards(n, ranks, x_emb, y_emb, q_factor, r_factor, g_weights, a_mass, b_mass, expr):
    rows, dim = x_emb.shape
    genes = expr.shape[1]
    rank_all = ranks * LANES
    owners = min(n // 2, dim // 16)
    groups = n // 2
    tiles = min(groups // 2, rank_all // 2 // (16 * HALVES))
    hbm = pl.BlockSpec(memory_space=pltpu.HBM)
    dma = pltpu.SemaphoreType.DMA
    pair = [dma((n,)), dma((n,))]
    single = [dma((1,)), dma((1,))]
    three = [dma((3,)), dma((3,))]
    lined = [dma((groups, HALVES)), dma((groups, HALVES))]
    block = (HALVES, rank_all // 2 // tiles // HALVES, genes)
    shapes = (
        jax.ShapeDtypeStruct(q_factor.shape, F32),
        jax.ShapeDtypeStruct(r_factor.shape, F32),
        jax.ShapeDtypeStruct((1, LANES), F32),
        jax.ShapeDtypeStruct((rows, genes), BF16),
    )
    results = pl.pallas_call(
        functools.partial(kernel, n, ranks, owners, tiles, float(rows * n)),
        out_shape=shapes,
        in_specs=[hbm] * 8,
        out_specs=(hbm,) * 4,
        scratch_shapes=[
            pltpu.VMEM(q_factor.shape, F32),
            pltpu.VMEM(r_factor.shape, F32),
            pltpu.VMEM((1, LANES), F32),
            pltpu.VMEM((rows, genes), BF16),
            dma((3 + BLOCKS,)),
            pltpu.VMEM(x_emb.shape, BF16),
            pltpu.VMEM(y_emb.shape, BF16),
            pltpu.VMEM(q_factor.shape, F32),
            pltpu.VMEM(r_factor.shape, F32),
            pltpu.VMEM((1, LANES), F32),
            pltpu.VMEM((1, rows), F32),
            pltpu.VMEM((1, rows), F32),
            pltpu.VMEM(expr.shape, BF16),
            dma((8,)),
            pltpu.VMEM((ranks, 2, rows, LANES), BF16),
            pltpu.VMEM((owners, 2, dim // owners, LANES), BF16),
            pltpu.VMEM((n, 2, dim // owners, LANES), BF16),
            pltpu.VMEM((ranks, owners, 2, dim // owners, LANES), BF16),
            pltpu.VMEM((n, 8, LANES), F32),
            pltpu.VMEM((ranks, 8, LANES), F32),
            pltpu.VMEM((ranks, rows, LANES), F32),
            pltpu.VMEM((ranks, rows, LANES), F32),
            pltpu.VMEM((ranks, 8, LANES), F32),
            pltpu.VMEM((ranks, 2, LANES, rows), BF16),
            pltpu.VMEM((ranks, 2, LANES, rows), F32),
            pltpu.VMEM((n, 8, LANES), F32),
            pltpu.VMEM((rows, rank_all), BF16),
            pltpu.VMEM((rows, rank_all), BF16),
            pltpu.VMEM((rank_all, rows), BF16),
            pltpu.VMEM((2, rank_all // 2, rows), BF16),
            pltpu.VMEM((2, n, 8, LANES), F32),
            pltpu.VMEM((rank_all // 2, rows), BF16),
            pltpu.VMEM(expr.shape, BF16),
            pltpu.VMEM((2, 1, rows), F32),
            pltpu.VMEM((2, rows, rank_all // 2), BF16),
            pltpu.VMEM((tiles,) + block, BF16),
            pltpu.VMEM((groups,) + block, BF16),
            pltpu.VMEM((2, tiles) + block, BF16),
        ]
        + pair + single + pair + three
        + [dma((3, owners)), dma((3, owners))]
        + three + single
        + [dma((2,)), dma((2,))]
        + [dma((3, PIECES)), dma((3, PIECES))]
        + lined + lined + lined,
        compiler_params=pltpu.CompilerParams(
            collective_id=0, has_side_effects=True, vmem_limit_bytes=VMEM_LIMIT
        ),
        cost_estimate=pl.CostEstimate(
            flops=2 * rows * (2 * dim * LANES + 2 * dim * rank_all + 2 * rank_all * genes),
            bytes_accessed=4 * 1024 * 1024,
            transcendentals=2 * rows * rank_all,
        ),
        name="transport_step",
    )(
        x_emb, y_emb, q_factor, r_factor, g_weights.reshape(1, LANES),
        a_mass.reshape(1, rows), b_mass.reshape(1, rows), expr,
    )
    q_new, r_new, rank_share, predicted = pl.pallas_call(
        functools.partial(write_out, len(shapes)),
        out_shape=shapes,
        in_specs=[hbm] * 4,
        out_specs=(hbm,) * 4,
        scratch_shapes=[pltpu.VMEM(shape.shape, shape.dtype) for shape in shapes]
        + [dma((len(shapes) * BLOCKS,)), dma((len(shapes) * BLOCKS,))],
        compiler_params=pltpu.CompilerParams(vmem_limit_bytes=VMEM_LIMIT),
        name="write_out",
    )(*results)
    return q_new, r_new, rank_share.reshape(LANES), predicted


def solution(mesh):
    n, ranks = mesh.shape["cells"], mesh.shape["rank"]
    assert ranks == 4
    return jax.shard_map(
        functools.partial(shards, n, ranks),
        mesh=mesh,
        in_specs=(
            P("cells", None),
            P("cells", None),
            P("cells", "rank"),
            P("cells", "rank"),
            P("rank"),
            P("cells"),
            P("cells"),
            P("cells", "rank"),
        ),
        out_specs=(P("cells", "rank"), P("cells", "rank"), P("rank"), P("cells", "rank")),
        check_vma=False,
    )
```

```python
import functools

import jax
import jax.numpy as jnp
from jax import lax
from jax.experimental import pallas as pl
from jax.experimental.pallas import tpu as pltpu
from jax.sharding import PartitionSpec as P

PASSES = 10
PIECES = 8
BLOCKS = 4
HALVES = 2
SCALE = 0.0625
GAMMA = 10.0
POWER = 0.8
LANES = 128
VMEM_LIMIT = 56 * 1024 * 1024
MESH = pl.DeviceIdType.MESH
F32 = jnp.float32
BF16 = jnp.bfloat16


def dot(left, right):
    return jnp.dot(left, right, preferred_element_type=F32)


def contract_rows(left, right):
    return lax.dot_general(
        left, right, (((0,), (0,)), ((), ())), preferred_element_type=F32
    )


def wide(rows, first, count):
    return jnp.concatenate([rows[first + i : first + i + 1] for i in range(count)], axis=1)


def tall(*rows):
    return jnp.concatenate(
        [row[:, i * LANES : (i + 1) * LANES] for row in rows for i in range(row.shape[1] // LANES)],
        axis=0,
    )


def row_product(row, matrix):
    high = row.astype(BF16).astype(F32)
    low = row - high
    shape = (16, row.shape[1])
    index = lax.broadcasted_iota(jnp.int32, shape, 0)
    parts = jnp.where(
        index == 0,
        jnp.broadcast_to(high, shape),
        jnp.where(index == 1, jnp.broadcast_to(low, shape), 0.0),
    )
    out = dot(parts.astype(BF16), matrix)
    return out[0:1] + out[1:2]


def as_column(row):
    return jnp.transpose(jnp.broadcast_to(row, (LANES, row.shape[1])))


def pick_row(rows, index):
    position = lax.broadcasted_iota(jnp.int32, rows.shape, 0)
    return jnp.sum(jnp.where(position == index, rows, 0.0), axis=0, keepdims=True)


def kernel(
    n, ranks, owners, tiles, cells_total,
    x_hbm, y_hbm, q_hbm, r_hbm, g_hbm, a_hbm, b_hbm, expr_hbm,
    q_hbm_out, r_hbm_out, w_hbm_out, pred_hbm_out,
    q_out, r_out, w_out, pred_out, out_sem,
    x_ref, y_ref, q_ref, r_ref, g_ref, a_ref, b_ref, expr_ref, in_sem,
    factors, part_src, part_buf, cross, vec_buf, vecs, grads_q, grads_r, grads_g,
    peaks, kq, kr, kqt, krt, t_buf, mate_kern, mate_expr, u_buf, scaled,
    prof_src, prof_buf, prof,
    part_send, part_recv, vec_send, vec_recv, cross_send, cross_recv,
    fac_send, fac_recv, rank_send, rank_recv, vr_send, vr_recv,
    peak_send, peak_recv, t_send, t_recv, mate_send, mate_recv,
    prof_send, prof_recv, gat_send, gat_recv, fwd_send, fwd_recv,
):
    me = lax.axis_index("cells")
    k = lax.axis_index("rank")
    near = k + 1 - 2 * lax.rem(k, 2)
    far = lax.rem(k + 2, 4)
    across = 3 - k
    group, half = me // 2, lax.rem(me, 2)
    groups = n // 2
    mate = me + 1 - 2 * half

    def each(first, last, body):
        if last - first <= 8:
            for i in range(first, last):
                body(i)
        else:
            def one(i, carry):
                body(i)
                return carry
            lax.fori_loop(first, last, one, 0)

    def others(index, count):
        if count > 8 or count & (count - 1):
            return lambda body, reverse=False: each(
                1, count, lambda offset: body(lax.rem(index + offset, count))
            )
        found = []
        for offset in range(count - 1, 0, -1):
            other = index
            for bit in (1, 2, 4):
                if offset & bit:
                    other = other + bit - 2 * bit * lax.rem(index // bit, 2)
            found.append(other)

        def over(body, reverse=False):
            for other in found[::-1] if reverse else found:
                body(other)

        return over

    peers = others(me, n)
    lines = others(group, groups)

    first, line_first = (n - owners) // 2, (groups - tiles) // 2
    mine, line_mine = me - first, group - line_first

    def owner(body):
        pl.when((me >= first) & (me < first + owners))(body)

    def line_owner(body):
        pl.when((group >= line_first) & (group < line_first + tiles))(body)

    def other_owners(body):
        each(0, owners, lambda o: pl.when(first + o != me)(functools.partial(body, o)))

    def other_line_owners(body):
        each(0, tiles, lambda o: pl.when(line_first + o != group)(functools.partial(body, o)))

    def to_peer(src, dst, send, recv, j):
        return pltpu.make_async_remote_copy(
            src_ref=src, dst_ref=dst, send_sem=send, recv_sem=recv,
            device_id=(j, k), device_id_type=MESH,
        )

    def to_rank(src, dst, send, recv, other):
        return pltpu.make_async_remote_copy(
            src_ref=src, dst_ref=dst, send_sem=send, recv_sem=recv,
            device_id=(me, other), device_id_type=MESH,
        )

    def all_copies(slots, send, recv):
        most = slots.at[pl.ds(0, n - 1)]
        return to_peer(most, most, send, recv, mate)

    barrier = pltpu.get_barrier_semaphore()
    peers(lambda j: pl.semaphore_signal(barrier, inc=1, device_id=(j, k), device_id_type=MESH))
    for other in (near, far, across):
        pl.semaphore_signal(barrier, inc=1, device_id=(me, other), device_id_type=MESH)

    loads = [
        pltpu.make_async_copy(src, dst, in_sem.at[i])
        for i, (src, dst) in enumerate(
            (
                (q_hbm, q_ref), (x_hbm, x_ref), (r_hbm, r_ref), (y_hbm, y_ref),
                (g_hbm, g_ref), (a_hbm, a_ref), (b_hbm, b_ref), (expr_hbm, expr_ref),
            )
        )
    ]
    for load in loads:
        load.start()
    depth = part_src.shape[2]
    loads[0].wait()
    q = q_ref[...]
    q_round = q.astype(BF16)
    factors[k, 0] = q_round
    loads[1].wait()
    x = x_ref[...]
    part_src[:, 0] = contract_rows(x, q_round).astype(BF16).reshape(owners, depth, LANES)
    loads[2].wait()
    r = r_ref[...]
    r_round = r.astype(BF16)
    factors[k, 1] = r_round
    loads[3].wait()
    y = y_ref[...]
    part_src[:, 1] = contract_rows(y, r_round).astype(BF16).reshape(owners, depth, LANES)
    for load in loads[4:]:
        load.wait()
    pl.semaphore_wait(barrier, n - 1 + 3)

    def part_copy(o):
        return to_peer(
            part_src.at[o], part_buf.at[me], part_send.at[o], part_recv.at[me], first + o
        )

    def part_arrival(j):
        return to_peer(part_src.at[0], part_buf.at[j], part_send.at[0], part_recv.at[j], j)

    def vec_copy(j, slot):
        return to_peer(vec_buf.at[me], vec_buf.at[slot], vec_send.at[0], vec_recv.at[0], j)

    other_owners(lambda o: part_copy(o).start())

    def factor_copy(slot, i, other):
        return to_rank(factors.at[slot], factors.at[slot], fac_send.at[i], fac_recv.at[i], other)

    factor_copy(k, 0, near).start()
    factor_copy(k, 1, far).start()

    norms_one = jnp.sum(jnp.square(x.astype(F32)), axis=1, keepdims=True)
    norms_two = jnp.sum(jnp.square(y.astype(F32)), axis=1, keepdims=True)
    vec_buf[me] = jnp.concatenate(
        [
            jnp.sum(norms_one * q, axis=0, keepdims=True),
            jnp.sum(q, axis=0, keepdims=True),
            jnp.sum(norms_two * r, axis=0, keepdims=True),
            jnp.sum(r, axis=0, keepdims=True),
            jnp.zeros((4, LANES), F32),
        ],
        axis=0,
    )
    peers(lambda j: vec_copy(j, me).start())

    def cross_copy(j, o):
        return to_peer(cross.at[k, o], cross.at[k, o], cross_send.at[j], cross_recv.at[o], j)

    def rank_copy(slot, i, other, j):
        return to_rank(
            cross.at[slot, j], cross.at[slot, j], rank_send.at[i, j], rank_recv.at[i, j], other
        )

    def pass_on(j):
        rank_copy(k, 2, across, j).start()
        rank_copy(k, 1, far, j).start()
        rank_copy(k, 0, near, j).start()

    @owner
    def reduce_parts():
        part_buf[me] = part_src[mine]
        peers(lambda j: part_arrival(j).wait_recv())
        total = part_buf[0].astype(F32)
        for j in range(1, n):
            total = total + part_buf[j].astype(F32)
        cross[k, mine] = total.astype(BF16)
        peers(lambda j: cross_copy(j, mine).start())
        pass_on(mine)

    all_copies(vec_buf, vec_send.at[0], vec_recv.at[0]).wait_recv()
    vec = vec_buf[0]
    for j in range(1, n):
        vec = vec + vec_buf[j]
    slot_row = lax.broadcasted_iota(jnp.int32, (8, LANES), 0)
    vecs[k] = jnp.where(slot_row == 4, jnp.broadcast_to(g_ref[...], (8, LANES)), vec)

    def vecs_copy(slot, i, other):
        return to_rank(vecs.at[slot], vecs.at[slot], vr_send.at[i], vr_recv.at[i], other)

    for i, other in enumerate((near, far, across)):
        vecs_copy(k, i, other).start()

    def arrived(o):
        cross_copy(first + o, o).wait_recv()
        pass_on(o)

    other_owners(arrived)
    factor_copy(far, 1, far).wait_recv()
    factor_copy(far, 2, near).start()

    def expr_copy(piece):
        size = expr_ref.shape[0] // PIECES
        rows = pl.ds(pl.multiple_of(piece * size, size), size)
        return to_peer(
            expr_ref.at[rows], mate_expr.at[rows], mate_send.at[0, piece], mate_recv.at[0, piece], mate
        )

    def kern_copy(piece):
        size = mate_kern.shape[0] // PIECES
        rows = pl.ds(pl.multiple_of(piece * size, size), size)
        return to_peer(
            krt.at[1 - half, rows], mate_kern.at[rows],
            mate_send.at[1, piece], mate_recv.at[1, piece], mate,
        )

    u_copy = to_peer(u_buf.at[0], u_buf.at[1], mate_send.at[2, 0], mate_recv.at[2, 0], mate)

    def gradients(kk):
        info = vecs[kk]
        xq_vec, cq_vec, yr_vec, cr_vec, g = (info[i : i + 1] for i in range(5))
        scale = SCALE / g
        dim = x.shape[1]
        cross_xq = cross[kk, :, 0].reshape(dim, LANES)
        cross_yr = cross[kk, :, 1].reshape(dim, LANES)
        grad_q = (norms_one * cr_vec + yr_vec - 2.0 * dot(x, cross_yr)) * scale
        grad_r = (norms_two * cq_vec + xq_vec - 2.0 * dot(y, cross_xq)) * scale
        grads_q[kk] = grad_q
        grads_r[kk] = grad_r
        inner = jnp.sum(cross_xq.astype(F32) * cross_yr.astype(F32), axis=0, keepdims=True)
        curvature = SCALE * (xq_vec * cr_vec + cq_vec * yr_vec - 2.0 * inner)
        grad_g = -curvature / jnp.square(g)
        grads_g[kk] = jnp.broadcast_to(grad_g, (8, LANES))
        return jnp.maximum(
            jnp.max(jnp.maximum(jnp.abs(grad_q), jnp.abs(grad_r)), axis=0, keepdims=True),
            jnp.abs(grad_g),
        )

    peak = gradients(k)
    vecs_copy(near, 0, near).wait_recv()
    each(0, owners, lambda j: rank_copy(near, 0, near, j).wait_recv())
    peak = jnp.maximum(peak, gradients(near))
    each(0, owners, lambda j: rank_copy(far, 1, far, j).wait_recv())
    vecs_copy(far, 1, far).wait_recv()
    peak = jnp.maximum(peak, gradients(far))
    vecs_copy(across, 2, across).wait_recv()
    each(0, owners, lambda j: rank_copy(across, 2, across, j).wait_recv())
    peak = jnp.maximum(peak, gradients(across))
    peaks[me] = jnp.broadcast_to(peak, (8, LANES))

    def peak_copy(j, slot):
        return to_peer(peaks.at[me], peaks.at[slot], peak_send.at[0], peak_recv.at[0], j)

    peers(lambda j: peak_copy(j, me).start())
    factor_copy(near, 0, near).wait_recv()
    factor_copy(across, 2, near).wait_recv()
    log_a, log_b = jnp.log(a_ref[...]), jnp.log(b_ref[...])
    all_copies(peaks, peak_send.at[0], peak_recv.at[0]).wait_recv()
    top = peaks[0]
    for j in range(1, n):
        top = jnp.maximum(top, peaks[j])
    eta = GAMMA / (jnp.max(top, axis=1, keepdims=True)[0:1] + 1e-6)

    log_g = []
    for kk in range(ranks):
        columns = slice(kk * LANES, (kk + 1) * LANES)
        kern_q = factors[kk, 0].astype(F32) * jnp.exp(-eta * grads_q[kk])
        kern_r = factors[kk, 1].astype(F32) * jnp.exp(-eta * grads_r[kk])
        kern_q, kern_r = kern_q.astype(BF16), kern_r.astype(BF16)
        kq[:, columns] = kern_q
        kr[:, columns] = kern_r
        kqt[columns, :] = jnp.transpose(kern_q)
        rows = slice(kk % 2 * LANES, (kk % 2 + 1) * LANES)
        krt[kk // 2, rows, :] = jnp.transpose(kern_r)
        log_g.append(jnp.log(vecs[kk][4:5]) - eta * grads_g[kk][0:1])
    log_kern_g = jnp.concatenate(log_g + log_g, axis=0)

    def t_copy(parity, j, slot):
        return to_peer(
            t_buf.at[parity, me], t_buf.at[parity, slot],
            t_send.at[parity], t_recv.at[parity], j,
        )

    def t_all(parity):
        return all_copies(t_buf.at[parity], t_send.at[parity], t_recv.at[parity])

    def whole_krt():
        return krt[...].reshape(ranks * LANES, krt.shape[2])

    def marginals(v):
        s_r = row_product(wide(v, ranks, ranks), whole_krt())
        u_r = jnp.exp(POWER * (log_b - jnp.log(s_r)))
        s_q = row_product(wide(v, 0, ranks), kqt[...])
        u_q = jnp.exp(POWER * (log_a - jnp.log(s_q)))
        return u_q, u_r

    def send_t(parity, u_q, u_r):
        t_buf[parity, me] = tall(row_product(u_q, kq[...]), row_product(u_r, kr[...]))
        peers(lambda j: t_copy(parity, j, me).start())

    def new_weights(parity, v):
        t_all(parity).wait_recv()
        t = t_buf[parity, 0]
        for j in range(1, n):
            t = t + t_buf[parity, j]
        t_all(parity).wait_send()
        logs = jnp.log(v * t)
        other = jnp.concatenate([logs[ranks:], logs[:ranks]], axis=0)
        weights = jnp.exp((log_kern_g + logs + other) / 3.0)
        return weights / t, weights, t

    def one_pass(step, v):
        parity = lax.rem(step, 2)
        send_t(parity, *marginals(v))

        @pl.when(step < PIECES)
        def send_piece():
            expr_copy(step).start()
            kern_copy(step).start()

        return new_weights(parity, v)[0]

    v = lax.fori_loop(0, PASSES - 1, one_pass, jnp.ones((2 * ranks, LANES), F32))
    u_q, u_r = marginals(v)
    u_buf[0] = u_r
    u_copy.start()
    send_t((PASSES - 1) % 2, u_q, u_r)

    def prof_copy(o, piece):
        return to_peer(
            prof_src.at[o, piece], prof_buf.at[group, piece],
            prof_send.at[o, piece], prof_recv.at[group, piece], 2 * (line_first + o) + half,
        )

    def prof_arrival(line, piece):
        return to_peer(
            prof_src.at[0, piece], prof_buf.at[line, piece],
            prof_send.at[0, piece], prof_recv.at[line, piece], 2 * line + half,
        )

    left = (krt[half].astype(F32) * u_r).astype(BF16)
    total = dot(left, expr_ref[...])
    for piece in range(PIECES):
        expr_copy(piece).wait_recv()
        kern_copy(piece).wait_recv()
    u_copy.wait_recv()
    left = (mate_kern[...].astype(F32) * u_buf[1]).astype(BF16)
    total = total + dot(left, mate_expr[...])
    prof_src[...] = total.astype(BF16).reshape(prof_src.shape)
    for piece in range(HALVES):
        other_line_owners(lambda o: prof_copy(o, piece).start())

    @line_owner
    def own_prof():
        prof_buf[group] = prof_src[line_mine]

    v, weights, t = new_weights((PASSES - 1) % 2, v)

    other_owners(lambda o: part_copy(o).wait_send())

    @owner
    def cross_sends():
        peers(lambda j: cross_copy(j, mine).wait_send())

    all_copies(vec_buf, vec_send.at[0], vec_recv.at[0]).wait_send()
    all_copies(peaks, peak_send.at[0], peak_recv.at[0]).wait_send()
    for i, (slot, other) in enumerate(((k, near), (k, far), (far, near))):
        factor_copy(slot, i, other).wait_send()
    for i, other in enumerate((near, far, across)):
        each(0, owners, lambda j: rank_copy(k, i, other, j).wait_send())
        vecs_copy(k, i, other).wait_send()
    u_copy.wait_send()
    for piece in range(PIECES):
        expr_copy(piece).wait_send()
        kern_copy(piece).wait_send()
    w_out[...] = pick_row(weights, k) / cells_total
    own_q = q_ref[...] * jnp.exp(-eta * grads_q[k])
    own_r = r_ref[...] * jnp.exp(-eta * grads_r[k])
    q_out[...] = as_column(u_q) * own_q * pick_row(v, k)
    r_out[...] = as_column(u_r) * own_r * pick_row(v, k + ranks)
    def block_rows(i):
        size = pred_out.shape[0] // BLOCKS
        return slice(i * size, (i + 1) * size)

    stores = [
        pltpu.make_async_copy(src, dst, out_sem.at[i])
        for i, (src, dst) in enumerate(
            (
                (q_out, q_hbm_out), (r_out, r_hbm_out),
                (w_out, w_hbm_out),
            )
            + tuple(
                (pred_out.at[block_rows(i)], pred_hbm_out.at[block_rows(i)])
                for i in range(BLOCKS)
            )
        )
    ]
    for store in stores[:3]:
        store.start()
    inverse = as_column(1.0 / row_product(wide(v, 0, ranks), kqt[...]))
    ratio = wide(v[ranks:] / t[:ranks], 0, ranks)
    width = scaled.shape[2]
    for i in range(2):
        columns = slice(i * width, (i + 1) * width)
        scaled[i] = (kq[:, columns].astype(F32) * ratio[:, columns]).astype(BF16)

    def gather_copy(line, o, piece):
        return to_peer(
            prof.at[half, o, piece], prof.at[half, o, piece],
            gat_send.at[line, piece], gat_recv.at[o, piece], 2 * line + half,
        )

    def forward_copy(side, o, piece):
        return to_peer(
            prof.at[side, o, piece], prof.at[side, o, piece],
            fwd_send.at[o, piece], fwd_recv.at[o, piece], mate,
        )

    @line_owner
    def reduce_prof():
        for piece in range(HALVES):
            lines(lambda line: prof_arrival(line, piece).wait_recv())
            total = prof_buf[0, piece].astype(F32)
            for line in range(1, groups):
                total = total + prof_buf[line, piece].astype(F32)
            prof[half, line_mine, piece] = total.astype(BF16)
            lines(lambda line: gather_copy(line, line_mine, piece).start())
            forward_copy(half, line_mine, piece).start()

    def gathered(o, piece):
        gather_copy(line_first + o, o, piece).wait_recv()
        forward_copy(half, o, piece).start()

    for piece in range(HALVES):
        other_line_owners(lambda o: gathered(o, piece))
    flat = (scaled.shape[2], prof.shape[4])
    for piece in range(HALVES):
        each(0, tiles, lambda o: forward_copy(1 - half, o, piece).wait_recv())
    for i in range(BLOCKS):
        rows = block_rows(i)
        mixed = dot(scaled[half, rows], prof[half].reshape(flat))
        mixed = mixed + dot(scaled[1 - half, rows], prof[1 - half].reshape(flat))
        across_genes = jnp.concatenate([inverse[rows]] * (mixed.shape[1] // LANES), axis=1)
        pred_out[rows] = (mixed * across_genes).astype(BF16)
        stores[3 + i].start()

    for piece in range(HALVES):
        other_line_owners(lambda o: prof_copy(o, piece).wait_send())
        each(0, tiles, lambda o: forward_copy(half, o, piece).wait_send())

    @line_owner
    def gather_sends():
        for piece in range(HALVES):
            lines(lambda line: gather_copy(line, line_mine, piece).wait_send())

    for store in stores:
        store.wait()


def write_out(count, *refs):
    sources, results, held = (refs[i * count : (i + 1) * count] for i in range(3))
    load_sem, store_sem = refs[3 * count :]
    loads, stores = [], []
    for source, result, hold in zip(sources, results, held):
        pieces = BLOCKS if source.shape[0] > BLOCKS else 1
        size = source.shape[0] // pieces
        for i in range(pieces):
            rows = pl.ds(i * size, size)
            sem = len(loads)
            loads.append(
                pltpu.make_async_copy(source.at[rows], hold.at[rows], load_sem.at[sem])
            )
            stores.append(
                pltpu.make_async_copy(hold.at[rows], result.at[rows], store_sem.at[sem])
            )
    for load in loads:
        load.start()
    for load, store in zip(loads, stores):
        load.wait()
        store.start()
    for store in stores:
        store.wait()


def shards(n, ranks, x_emb, y_emb, q_factor, r_factor, g_weights, a_mass, b_mass, expr):
    rows, dim = x_emb.shape
    genes = expr.shape[1]
    rank_all = ranks * LANES
    owners = min(n // 2, dim // 16)
    groups = n // 2
    tiles = min(groups // 2, rank_all // 2 // (16 * HALVES))
    hbm = pl.BlockSpec(memory_space=pltpu.HBM)
    dma = pltpu.SemaphoreType.DMA
    pair = [dma((n,)), dma((n,))]
    single = [dma((1,)), dma((1,))]
    three = [dma((3,)), dma((3,))]
    lined = [dma((groups, HALVES)), dma((groups, HALVES))]
    block = (HALVES, rank_all // 2 // tiles // HALVES, genes)
    shapes = (
        jax.ShapeDtypeStruct(q_factor.shape, F32),
        jax.ShapeDtypeStruct(r_factor.shape, F32),
        jax.ShapeDtypeStruct((1, LANES), F32),
        jax.ShapeDtypeStruct((rows, genes), BF16),
    )
    results = pl.pallas_call(
        functools.partial(kernel, n, ranks, owners, tiles, float(rows * n)),
        out_shape=shapes,
        in_specs=[hbm] * 8,
        out_specs=(hbm,) * 4,
        scratch_shapes=[
            pltpu.VMEM(q_factor.shape, F32),
            pltpu.VMEM(r_factor.shape, F32),
            pltpu.VMEM((1, LANES), F32),
            pltpu.VMEM((rows, genes), BF16),
            dma((3 + BLOCKS,)),
            pltpu.VMEM(x_emb.shape, BF16),
            pltpu.VMEM(y_emb.shape, BF16),
            pltpu.VMEM(q_factor.shape, F32),
            pltpu.VMEM(r_factor.shape, F32),
            pltpu.VMEM((1, LANES), F32),
            pltpu.VMEM((1, rows), F32),
            pltpu.VMEM((1, rows), F32),
            pltpu.VMEM(expr.shape, BF16),
            dma((8,)),
            pltpu.VMEM((ranks, 2, rows, LANES), BF16),
            pltpu.VMEM((owners, 2, dim // owners, LANES), BF16),
            pltpu.VMEM((n, 2, dim // owners, LANES), BF16),
            pltpu.VMEM((ranks, owners, 2, dim // owners, LANES), BF16),
            pltpu.VMEM((n, 8, LANES), F32),
            pltpu.VMEM((ranks, 8, LANES), F32),
            pltpu.VMEM((ranks, rows, LANES), F32),
            pltpu.VMEM((ranks, rows, LANES), F32),
            pltpu.VMEM((ranks, 8, LANES), F32),
            pltpu.VMEM((n, 8, LANES), F32),
            pltpu.VMEM((rows, rank_all), BF16),
            pltpu.VMEM((rows, rank_all), BF16),
            pltpu.VMEM((rank_all, rows), BF16),
            pltpu.VMEM((2, rank_all // 2, rows), BF16),
            pltpu.VMEM((2, n, 8, LANES), F32),
            pltpu.VMEM((rank_all // 2, rows), BF16),
            pltpu.VMEM(expr.shape, BF16),
            pltpu.VMEM((2, 1, rows), F32),
            pltpu.VMEM((2, rows, rank_all // 2), BF16),
            pltpu.VMEM((tiles,) + block, BF16),
            pltpu.VMEM((groups,) + block, BF16),
            pltpu.VMEM((2, tiles) + block, BF16),
        ]
        + pair + single + pair + three
        + [dma((3, owners)), dma((3, owners))]
        + three + single
        + [dma((2,)), dma((2,))]
        + [dma((3, PIECES)), dma((3, PIECES))]
        + lined + lined + lined,
        compiler_params=pltpu.CompilerParams(
            collective_id=0, has_side_effects=True, vmem_limit_bytes=VMEM_LIMIT
        ),
        cost_estimate=pl.CostEstimate(
            flops=2 * rows * (2 * dim * LANES + 2 * dim * rank_all + 2 * rank_all * genes),
            bytes_accessed=4 * 1024 * 1024,
            transcendentals=2 * rows * rank_all,
        ),
        name="transport_step",
    )(
        x_emb, y_emb, q_factor, r_factor, g_weights.reshape(1, LANES),
        a_mass.reshape(1, rows), b_mass.reshape(1, rows), expr,
    )
    q_new, r_new, rank_share, predicted = pl.pallas_call(
        functools.partial(write_out, len(shapes)),
        out_shape=shapes,
        in_specs=[hbm] * 4,
        out_specs=(hbm,) * 4,
        scratch_shapes=[pltpu.VMEM(shape.shape, shape.dtype) for shape in shapes]
        + [dma((len(shapes) * BLOCKS,)), dma((len(shapes) * BLOCKS,))],
        compiler_params=pltpu.CompilerParams(vmem_limit_bytes=VMEM_LIMIT),
        name="write_out",
    )(*results)
    return q_new, r_new, rank_share.reshape(LANES), predicted


def solution(mesh):
    n, ranks = mesh.shape["cells"], mesh.shape["rank"]
    assert ranks == 4
    return jax.shard_map(
        functools.partial(shards, n, ranks),
        mesh=mesh,
        in_specs=(
            P("cells", None),
            P("cells", None),
            P("cells", "rank"),
            P("cells", "rank"),
            P("rank"),
            P("cells"),
            P("cells"),
            P("cells", "rank"),
        ),
        out_specs=(P("cells", "rank"), P("cells", "rank"), P("rank"), P("cells", "rank")),
        check_vma=False,
    )
```
